256 devices in a mesh: lat: 16 (over z, core), lon: 16 (over x, y).
Axes of the slice: x: 4, y: 4, z: 8, core: 2. Of those that a mesh axis runs over, the one named last changes fastest.
Arguments:
- grid_values: float32 [768, 1440, 256], P('lat', 'lon'), may hold values from -6 to 6
- wave_table: int32 [512], replicated, may hold values from 0 to 511, as said below
- legendre_basis: float32 [512, 384, 720], P(('lat', 'lon')), as said below
Outputs:
- coefficients: float32 [512, 720, 512], P(('lat', 'lon'))
The draws below stay inside these ranges and needn't reach their ends.
Inputs may be any that keep to these rules, and one draw needn't show every extreme that they name: `wave_table`: a permutation of the wavenumbers 0 to 511. legendre_basis[r, j, l] is zero wherever l < wave_table[r].
All inputs are finite; a program needn't handle non-finite values.
Results may differ from the reference program's by a relative error of at most 0.0003.
Values sent between devices are 32-bit elements; how exact they have to be, the bound alone decides.
A program may use at most 128 MiB of HBM per device.

```python
import math
import jax
import jax.numpy as jnp
from jax import lax

CHANNELS = 256
NLON = 1440
MMAX = 512
LMAX = 720
NLAT = 768


def common_table(key):
    return jax.random.permutation(key, MMAX).astype(jnp.int32)


def draw_wave_table(key, part):
    return common_table(key)


def draw_legendre_basis(key, part):
    waves = common_table(key)
    key = jax.random.fold_in(key, 11)
    shape = (MMAX, NLAT // 2, LMAX)
    values = jax.random.normal(key, shape, jnp.float32)
    degrees = jnp.arange(LMAX, dtype=jnp.int32)
    keep = degrees[None, None, :] >= waves[:, None, None]
    return jnp.where(keep, values / jnp.sqrt(jnp.float32(NLAT)), 0.0).astype(jnp.float32)


def level_of(own_key, dims, shards, smallest, high):
    def one(position, blocks):
        steps = jax.random.uniform(jax.random.fold_in(jax.random.fold_in(own_key, 6), position), (blocks,), jnp.float32, smallest / len(shards), high / len(shards))
        return jnp.repeat(jnp.exp(steps), dims[position] // blocks).reshape((-1,) + (1,) * (len(dims) - position - 1))

    level = one(*shards[0])
    for cut in shards[1:]:
        level = level * one(*cut)
    return level


def centred(stream_key, extent, width, bound, cuts=(), held_as=jnp.bfloat16):
    gain = level_of(stream_key, extent, cuts, -0.22, 0.18) if cuts else 1.0
    entries = jax.random.normal(stream_key, extent, jnp.float32) * width * gain
    return jnp.minimum(jnp.maximum(entries, -bound), bound).astype(held_as)


def setup_inputs(seed: int = 0) -> dict:
    key_list = jax.random.split(jax.random.key(seed), 4)
    return {
        "grid_values": centred(key_list[0], (NLAT, NLON, CHANNELS), 1.0, 6.0, ((0, 16), (1, 16)), jnp.float32),
        "wave_table": draw_wave_table(jax.random.fold_in(key_list[3], 71), 0),
        "legendre_basis": draw_legendre_basis(jax.random.fold_in(key_list[3], 71), 0),
    }


def reference(grid_values, wave_table, legendre_basis):
    spectrum = jnp.fft.rfft(grid_values, axis=1)[:, :MMAX] / math.sqrt(NLON)
    stacked = jnp.stack([jnp.real(spectrum), jnp.imag(spectrum)], axis=2)
    picked = jnp.take(stacked, wave_table, axis=1)
    ordered = jnp.transpose(picked, (1, 0, 2, 3))
    half_rows = NLAT // 2
    southern = jnp.flip(ordered[:, half_rows:], axis=1)
    even_part = ordered[:, :half_rows] + southern
    odd_part = ordered[:, :half_rows] - southern
    group = 16
    degrees = jnp.arange(LMAX, dtype=jnp.int32)

    def one_group(operands):
        basis_part, even_one, odd_one, waves = operands
        even_sums = jnp.einsum('tjl,tjsc->tlsc', basis_part, even_one, precision=lax.Precision.HIGHEST)
        odd_sums = jnp.einsum('tjl,tjsc->tlsc', basis_part, odd_one, precision=lax.Precision.HIGHEST)
        flag = ((degrees[None, :] + waves[:, None]) % 2 == 0)[:, :, None, None]
        return jnp.where(flag, even_sums, odd_sums).reshape(group, LMAX, 2 * CHANNELS)
    groups = MMAX // group
    result = lax.map(one_group, (legendre_basis.reshape(groups, group, half_rows, LMAX), even_part.reshape(groups, group, half_rows, 2, CHANNELS), odd_part.reshape(groups, group, half_rows, 2, CHANNELS), wave_table.reshape(groups, group)))
    return result.reshape(MMAX, LMAX, 2 * CHANNELS)
```

```python
import functools
import math

import jax
import jax.numpy as jnp
from jax import lax
from jax.experimental import pallas as pl
from jax.experimental.pallas import tpu as pltpu
from jax.sharding import PartitionSpec as P

CIRCLE = 1440
LANES = 128
SECTORS = 16
BANDS = 16
SECTOR_ROWS = 96
POINTS = SECTORS * SECTOR_ROWS
THIRDS = 3
HALVES = 2
CHUNKS = THIRDS * HALVES
BLOCK = 64
ALL_ROWS = 16 * BLOCK


def split(values):
    high = values.astype(jnp.bfloat16)
    low = (values - high.astype(jnp.float32)).astype(jnp.bfloat16)
    return high, low


def unit_circle(turns):
    half = turns * math.pi
    square = half * half
    sine = jnp.full_like(half, -1.0 / 39916800.0)
    for order in (9, 7, 5, 3, 1):
        sine = sine * square + (-1.0) ** (order // 2) / math.factorial(order)
    sine = sine * half
    cosine = jnp.full_like(half, 1.0 / 479001600.0)
    for order in (10, 8, 6, 4, 2, 0):
        cosine = cosine * square + (-1.0) ** (order // 2) / math.factorial(order)
    return 1.0 - 2.0 * sine * sine, 2.0 * sine * cosine


def fraction(product, circle):
    whole = jnp.floor(product * (1.0 / circle) + 0.5)
    return (product - whole * circle) * (1.0 / circle)


def kernel(
    grid, waves, basis, out,
    circles, matrix_high, matrix_low, points, send_lat, recv_lat, send_lon, recv_lon,
    table, table_high, table_low, total,
    sems, own_sems, local_sems, out_sems,
):
    lat = lax.axis_index("lat")
    lon = lax.axis_index("lon")
    place = jnp.where(lat < 8, lat, 23 - lat)
    basis_copy = pltpu.make_async_copy(basis, table, local_sems.at[0])
    basis_copy.start()

    barrier = pltpu.get_barrier_semaphore()

    def greet(step, _):
        pl.semaphore_signal(barrier, inc=1, device_id={"lon": lax.rem(lon + step, SECTORS)}, device_id_type=pl.DeviceIdType.MESH)
        pl.semaphore_signal(barrier, inc=1, device_id={"lat": lax.rem(lat + step, BANDS)}, device_id_type=pl.DeviceIdType.MESH)
        return 0

    lax.fori_loop(1, 16, greet, 0)
    pl.semaphore_wait(barrier, 30)

    def circle_row(third, owner):
        row = 16 * third + owner
        return jnp.where(lat < 8, row, 47 - row)

    def send_circles(chunk):
        half, third = divmod(chunk, THIRDS)
        lanes = pl.ds(half * LANES, LANES)

        def one(step, _):
            peer = lax.rem(lon + step, SECTORS)
            pltpu.make_async_remote_copy(
                src_ref=grid.at[circle_row(third, peer), :, lanes],
                dst_ref=circles.at[chunk, lon],
                send_sem=sems.at[0, chunk],
                recv_sem=sems.at[1, chunk],
                device_id={"lon": peer},
                device_id_type=pl.DeviceIdType.MESH,
            ).start()
            return 0

        lax.fori_loop(1, SECTORS, one, 0)
        pltpu.make_async_copy(grid.at[circle_row(third, lon), :, lanes], circles.at[chunk, lon], own_sems.at[0, chunk]).start()

    def wait_circles(chunk):
        most = circles.at[chunk, pl.ds(0, SECTORS - 1)]
        pltpu.make_async_copy(most, most, sems.at[1, chunk]).wait()
        one = circles.at[chunk, 0]
        pltpu.make_async_copy(one, one, own_sems.at[0, chunk]).wait()

    def send_blocks(stage, axis, me, my_place, source, target, chunk):
        def one(step, _):
            peer = lax.rem(me + step, 16)
            pltpu.make_async_remote_copy(
                src_ref=source.at[chunk, pl.ds(pl.multiple_of(peer * BLOCK, BLOCK), BLOCK)],
                dst_ref=target.at[chunk, pl.ds(pl.multiple_of(my_place * BLOCK, BLOCK), BLOCK)],
                send_sem=sems.at[2 * stage, chunk],
                recv_sem=sems.at[2 * stage + 1, chunk],
                device_id={axis: peer},
                device_id_type=pl.DeviceIdType.MESH,
            ).start()
            return 0

        lax.fori_loop(1, 16, one, 0)
        pltpu.make_async_copy(
            source.at[chunk, pl.ds(pl.multiple_of(me * BLOCK, BLOCK), BLOCK)],
            target.at[chunk, pl.ds(pl.multiple_of(my_place * BLOCK, BLOCK), BLOCK)],
            own_sems.at[stage, chunk],
        ).start()

    def wait_blocks(stage, target, chunk):
        most = target.at[chunk, pl.ds(0, 15 * BLOCK)]
        pltpu.make_async_copy(most, most, sems.at[2 * stage + 1, chunk]).wait()
        one = target.at[chunk, pl.ds(0, BLOCK)]
        pltpu.make_async_copy(one, one, own_sems.at[stage, chunk]).wait()

    def build_matrix():
        lane = lax.broadcasted_iota(jnp.int32, (32, LANES), 1).astype(jnp.float32)
        factor = 1.0 / math.sqrt(CIRCLE)

        def one(block, _):
            numbers = waves[pl.ds(pl.multiple_of(block * 32, 32), 32), :]
            for group in range(3):
                position = lane + float(LANES * group)
                sector = jnp.floor(position * (1.0 / 96.0) + 0.001)
                point = position - 6.0 * sector
                cosine, sine = unit_circle(fraction(numbers * point, float(CIRCLE)))
                cosine, sine = cosine * factor, sine * factor
                for quarter in range(4):
                    turn = fraction(numbers * float(quarter), 4.0) * 4.0
                    turn_cos = 1.0 - jnp.abs(turn)
                    turn_sin = jnp.where(turn == -2.0, 0.0, turn)
                    real = turn_cos * cosine - turn_sin * sine
                    imaginary = -turn_sin * cosine - turn_cos * sine
                    columns = pl.ds(384 * quarter + LANES * group, LANES)
                    for offset, values in ((0, real), (32, imaginary)):
                        rows = pl.ds(pl.multiple_of(block * BLOCK + offset, 32), 32)
                        matrix_high[rows, columns], matrix_low[rows, columns] = split(values)
            return 0

        lax.fori_loop(0, 16, one, 0)

    def build_table():
        degree = lax.broadcasted_iota(jnp.int32, (8, 720), 1).astype(jnp.float32)
        first = (lat * SECTORS + lon) * 2
        for slot in range(2):
            wave = waves[pl.ds(first + slot, 1), :][:, :1]
            sign = 1.0 - 4.0 * jnp.abs(fraction(degree + wave, 2.0))
            for third in range(THIRDS):
                rows = []
                for circle in range(16):
                    north = jnp.concatenate(
                        [table[slot, pl.ds(48 * band + 16 * third + circle, 1), :] for band in range(8)], 0
                    )
                    rows += [north, north * sign]
                stacked = jnp.concatenate(rows, 0)
                high, low = split(stacked.T)
                table_high[slot, third], table_low[slot, third] = high, low

    def transform(chunk):
        wait_circles(chunk)

        def cut(sector, _):
            values = circles[chunk, sector]
            values = jnp.concatenate([values, jnp.zeros((SECTOR_ROWS - 90, LANES), jnp.float32)], 0)
            high, low = split(values)
            rows = pl.ds(pl.multiple_of(sector * SECTOR_ROWS, SECTOR_ROWS), SECTOR_ROWS)
            points[rows, :LANES], points[rows, LANES:] = high, low
            return 0

        lax.fori_loop(0, SECTORS, cut, 0)

        def rows_of(part, _):
            rows = pl.ds(pl.multiple_of(part * 256, 256), 256)
            both = jnp.dot(matrix_high[rows, :], points[...], preferred_element_type=jnp.float32)
            rest = jnp.dot(matrix_low[rows, :], points[:, :LANES], preferred_element_type=jnp.float32)
            send_lat[chunk, rows, :] = both[:, :LANES] + both[:, LANES:] + rest
            return 0

        lax.fori_loop(0, 4, rows_of, 0)
        send_blocks(1, "lat", lat, place, send_lat, recv_lat, chunk)

    def turn_over(chunk):
        wait_blocks(1, recv_lat, chunk)

        def one(owner, _):
            for slot in range(2):
                for part in range(2):
                    values = recv_lat[chunk, pl.ds(part * 32 + owner * 2 + slot, 16, stride=BLOCK), :]
                    send_lon[chunk, pl.ds(pl.multiple_of(owner * BLOCK + slot * 32 + part * 16, 16), 16), :] = values
            return 0

        lax.fori_loop(0, SECTORS, one, 0)
        send_blocks(2, "lon", lon, lon, send_lon, recv_lon, chunk)

    def sum_up(chunk):
        half, third = divmod(chunk, THIRDS)
        wait_blocks(2, recv_lon, chunk)
        arrived = recv_lon[chunk].reshape(16, 2, 2, 16, LANES)
        for slot in range(2):
            pair = [arrived[:, slot, part].reshape(256, LANES) for part in range(2)]
            high, low = split(jnp.concatenate(pair, 1))
            one_high, one_low = table_high[slot, third], table_low[slot, third]
            sums = jnp.dot(one_high, high, preferred_element_type=jnp.float32)
            sums += jnp.dot(one_high, low, preferred_element_type=jnp.float32)
            sums += jnp.dot(one_low, high, preferred_element_type=jnp.float32)
            if third:
                sums += total[half, slot]
            total[half, slot] = sums
            if third == THIRDS - 1:
                for part in range(2):
                    out_copy(half, slot, part).start()

    def out_copy(half, slot, part):
        return pltpu.make_async_copy(
            total.at[half, slot, :, pl.ds(part * LANES, LANES)],
            out.at[slot, :, pl.ds(part * 256 + half * LANES, LANES)],
            out_sems.at[half, slot, part],
        )

    def wait_sent(stage, source, chunk):
        if stage == 0:
            most = circles.at[chunk, pl.ds(0, SECTORS - 1)]
        else:
            most = source.at[chunk, pl.ds(0, 15 * BLOCK)]
        pltpu.make_async_copy(most, most, sems.at[2 * stage, chunk]).wait()

    send_circles(0)
    send_circles(1)
    build_matrix()
    for step in range(CHUNKS + 2):
        if step < CHUNKS:
            transform(step)
            if step + 2 < CHUNKS:
                send_circles(step + 2)
            wait_sent(0, None, step)
        if step == 0:
            basis_copy.wait()
            build_table()
        if 1 <= step <= CHUNKS:
            turn_over(step - 1)
            wait_sent(1, send_lat, step - 1)
        if step >= 2:
            sum_up(step - 2)
            wait_sent(2, send_lon, step - 2)
    for half in range(HALVES):
        for slot in range(2):
            for part in range(2):
                out_copy(half, slot, part).wait()


def on_device(grid_values, wave_table, legendre_basis):
    waves = jnp.broadcast_to(wave_table.astype(jnp.float32)[:, None], (512, LANES))
    any_space = pl.BlockSpec(memory_space=pl.ANY)
    return pl.pallas_call(
        kernel,
        out_shape=jax.ShapeDtypeStruct((2, 720, 512), jnp.float32),
        in_specs=[any_space, pl.BlockSpec(memory_space=pltpu.VMEM), any_space],
        out_specs=any_space,
        scratch_shapes=[
            pltpu.VMEM((CHUNKS, SECTORS, 90, LANES), jnp.float32),
            pltpu.VMEM((ALL_ROWS, POINTS), jnp.bfloat16),
            pltpu.VMEM((ALL_ROWS, POINTS), jnp.bfloat16),
            pltpu.VMEM((POINTS, 2 * LANES), jnp.bfloat16),
            pltpu.VMEM((CHUNKS, ALL_ROWS, LANES), jnp.float32),
            pltpu.VMEM((CHUNKS, ALL_ROWS, LANES), jnp.float32),
            pltpu.VMEM((CHUNKS, ALL_ROWS, LANES), jnp.float32),
            pltpu.VMEM((CHUNKS, ALL_ROWS, LANES), jnp.float32),
            pltpu.VMEM((2, 384, 720), jnp.float32),
            pltpu.VMEM((2, THIRDS, 720, 256), jnp.bfloat16),
            pltpu.VMEM((2, THIRDS, 720, 256), jnp.bfloat16),
            pltpu.VMEM((HALVES, 2, 720, 256), jnp.float32),
            pltpu.SemaphoreType.DMA((6, CHUNKS)),
            pltpu.SemaphoreType.DMA((3, CHUNKS)),
            pltpu.SemaphoreType.DMA((2,)),
            pltpu.SemaphoreType.DMA((HALVES, 2, 2)),
        ],
        compiler_params=pltpu.CompilerParams(
            collective_id=0, has_side_effects=True, vmem_limit_bytes=56 * 1024 * 1024
        ),
        name="transform",
    )(grid_values, waves, legendre_basis)


def solution(mesh):
    placed = (P("lat", "lon", None), P(), P(("lat", "lon"), None, None))
    return jax.shard_map(
        on_device,
        mesh=mesh,
        in_specs=placed,
        out_specs=P(("lat", "lon"), None, None),
        check_vma=False,
    )
```

```python
import functools
import math

import jax
import jax.numpy as jnp
from jax import lax
from jax.experimental import pallas as pl
from jax.experimental.pallas import tpu as pltpu
from jax.sharding import PartitionSpec as P

CIRCLE = 1440
LANES = 128
SECTORS = 16
BANDS = 16
SECTOR_ROWS = 96
POINTS = SECTORS * SECTOR_ROWS
THIRDS = 3
HALVES = 2
CHUNKS = THIRDS * HALVES
BLOCK = 64
ALL_ROWS = 16 * BLOCK


LON_STEPS = (
    (1, 0), (0, 1), (3, 0), (0, 3), (2, 1), (1, 2), (2, 3), (3, 2), (1, 1), (3, 3), (1, 3), (3, 1), (2, 0), (0, 2), (2, 2),
)
LAT_STEPS = (
    (1, 0), (7, 1), (2, 0), (6, 1), (3, 0), (5, 1), (4, 0), (4, 1), (7, 0), (1, 1), (6, 0), (2, 1), (5, 0), (3, 1), (0, 1),
)


def split(values):
    high = values.astype(jnp.bfloat16)
    low = (values - high.astype(jnp.float32)).astype(jnp.bfloat16)
    return high, low


def unit_circle(turns):
    half = turns * math.pi
    square = half * half
    sine = jnp.full_like(half, -1.0 / 39916800.0)
    for order in (9, 7, 5, 3, 1):
        sine = sine * square + (-1.0) ** (order // 2) / math.factorial(order)
    sine = sine * half
    cosine = jnp.full_like(half, 1.0 / 479001600.0)
    for order in (10, 8, 6, 4, 2, 0):
        cosine = cosine * square + (-1.0) ** (order // 2) / math.factorial(order)
    return 1.0 - 2.0 * sine * sine, 2.0 * sine * cosine


def fraction(product, circle):
    whole = jnp.floor(product * (1.0 / circle) + 0.5)
    return (product - whole * circle) * (1.0 / circle)


def kernel(
    grid, numbers, basis, out,
    rows_held, circles_out, circles, waves, matrix_high, matrix_low, points,
    send_lat, recv_lat, send_lon, recv_lon,
    table, table_high, table_low,
    sems, own_sems, row_sems, table_sem,
):
    lat = lax.axis_index("lat")
    lon = lax.axis_index("lon")
    northern = lat < 8
    place = jnp.where(northern, lat, 23 - lat)

    core = lax.rem(lat, 2)
    turn = 1 - 2 * core

    def lon_peer(step, way):
        x = lax.rem(lon // 4 + way * turn * step[0] + 4, 4)
        y = lax.rem(lax.rem(lon, 4) + way * turn * step[1] + 4, 4)
        return x * 4 + y

    def lat_peer(step):
        z = lax.rem(lat // 2 + turn * step[0] + 8, 8)
        return z * 2 + lax.rem(core + step[1], 2)

    def load_rows(chunk):
        half, third = divmod(chunk, THIRDS)
        first = pl.multiple_of(jnp.where(northern, 16 * third, 32 - 16 * third), 16)
        return pltpu.make_async_copy(
            grid.at[:, pl.ds(first, 16), pl.ds(half * LANES, LANES)], rows_held.at[chunk], row_sems.at[chunk]
        )

    for chunk in range(CHUNKS):
        load_rows(chunk).start()
    table_copy = pltpu.make_async_copy(basis, table, table_sem)
    table_copy.start()

    barrier = pltpu.get_barrier_semaphore()

    def greet(step, _):
        pl.semaphore_signal(barrier, inc=1, device_id={"lon": lax.rem(lon + step, SECTORS)}, device_id_type=pl.DeviceIdType.MESH)
        pl.semaphore_signal(barrier, inc=1, device_id={"lat": lax.rem(lat + step, BANDS)}, device_id_type=pl.DeviceIdType.MESH)
        return 0

    lax.fori_loop(1, 16, greet, 0)

    def arrange(chunk, owner):
        start = jnp.where(northern, owner, 15 - owner)
        circles_out[chunk, owner] = rows_held.at[chunk].reshape(90 * 16, LANES)[pl.ds(start, 90, stride=16), :]

    def send_circle(chunk, peer):
        arrange(chunk, peer)
        pltpu.make_async_remote_copy(
            src_ref=circles_out.at[chunk, peer],
            dst_ref=circles.at[chunk, lon],
            send_sem=sems.at[0, chunk],
            recv_sem=sems.at[1, chunk],
            device_id={"lon": peer},
            device_id_type=pl.DeviceIdType.MESH,
        ).start()

    def keep_circle(chunk):
        arrange(chunk, lon)
        pltpu.make_async_copy(circles_out.at[chunk, lon], circles.at[chunk, lon], own_sems.at[0, chunk]).start()

    def wait_circles(chunk):
        most = circles.at[chunk, pl.ds(0, SECTORS - 1)]
        pltpu.make_async_copy(most, most, sems.at[1, chunk]).wait()
        one = circles.at[chunk, 0]
        pltpu.make_async_copy(one, one, own_sems.at[0, chunk]).wait()

    def block_copy(stage, peer, chunk):
        source, target = ((send_lat, recv_lat), (send_lon, recv_lon))[stage - 1]
        mine = (place, lon)[stage - 1]
        return (
            source.at[chunk, pl.ds(pl.multiple_of(peer * BLOCK, BLOCK), BLOCK)],
            target.at[chunk, pl.ds(pl.multiple_of(mine * BLOCK, BLOCK), BLOCK)],
        )

    def send_block(stage, peer, chunk):
        source, target = block_copy(stage, peer, chunk)
        pltpu.make_async_remote_copy(
            src_ref=source,
            dst_ref=target,
            send_sem=sems.at[2 * stage, chunk],
            recv_sem=sems.at[2 * stage + 1, chunk],
            device_id={("lat", "lon")[stage - 1]: peer},
            device_id_type=pl.DeviceIdType.MESH,
        ).start()

    def keep_block(stage, chunk):
        source, target = block_copy(stage, (lat, lon)[stage - 1], chunk)
        pltpu.make_async_copy(source, target, own_sems.at[stage, chunk]).start()

    def burst(circle_chunk=None, lat_chunk=None, lon_chunk=None):
        if circle_chunk:
            load_rows(circle_chunk).wait()
        for step in range(15):
            if lat_chunk is not None:
                send_block(1, lat_peer(LAT_STEPS[step]), lat_chunk)
            if circle_chunk is not None:
                send_circle(circle_chunk, lon_peer(LON_STEPS[step], 1))
            if lon_chunk is not None:
                send_block(2, lon_peer(LON_STEPS[step], -1), lon_chunk)
        if lat_chunk is not None:
            keep_block(1, lat_chunk)
        if circle_chunk is not None:
            keep_circle(circle_chunk)
        if lon_chunk is not None:
            keep_block(2, lon_chunk)

    def wait_blocks(stage, target, chunk):
        most = target.at[chunk, pl.ds(0, 15 * BLOCK)]
        pltpu.make_async_copy(most, most, sems.at[2 * stage + 1, chunk]).wait()
        one = target.at[chunk, pl.ds(0, BLOCK)]
        pltpu.make_async_copy(one, one, own_sems.at[stage, chunk]).wait()

    def spread_waves():
        for group in range(4):
            values = jnp.broadcast_to(numbers[group : group + 1, :].astype(jnp.float32), (LANES, LANES))
            waves[LANES * group : LANES * (group + 1), :] = values.T

    def build_matrix():
        lane = lax.broadcasted_iota(jnp.int32, (32, LANES), 1).astype(jnp.float32)
        factor = 1.0 / math.sqrt(CIRCLE)

        def one(block, _):
            wave = waves[pl.ds(pl.multiple_of(block * 32, 32), 32), :]
            for group in range(3):
                position = lane + float(LANES * group)
                sector = jnp.floor(position * (1.0 / 96.0) + 0.001)
                point = position - 6.0 * sector
                cosine, sine = unit_circle(fraction(wave * point, float(CIRCLE)))
                cosine, sine = cosine * factor, sine * factor
                for quarter in range(4):
                    turn = fraction(wave * float(quarter), 4.0) * 4.0
                    turn_cos = 1.0 - jnp.abs(turn)
                    turn_sin = jnp.where(turn == -2.0, 0.0, turn)
                    real = turn_cos * cosine - turn_sin * sine
                    imaginary = -turn_sin * cosine - turn_cos * sine
                    columns = pl.ds(384 * quarter + LANES * group, LANES)
                    for offset, values in ((0, real), (32, imaginary)):
                        rows = pl.ds(pl.multiple_of(block * BLOCK + offset, 32), 32)
                        matrix_high[rows, columns], matrix_low[rows, columns] = split(values)
            return 0

        lax.fori_loop(0, 16, one, 0)

    def build_table():
        table_copy.wait()
        degree = lax.broadcasted_iota(jnp.int32, (720, 256), 0).astype(jnp.float32)
        southern = (lax.broadcasted_iota(jnp.int32, (720, 256), 1) & 8) == 8
        row = lax.broadcasted_iota(jnp.int32, (384, 256), 0)
        column = lax.broadcasted_iota(jnp.int32, (384, 256), 1)
        wanted = 48 * (column & 7) + (column >> 4)
        first = (lat * SECTORS + lon) * 2
        for slot in range(2):
            wave = jnp.broadcast_to(waves[pl.ds(first + slot, 1), :][:, :1], (1, 256))
            sign = 1.0 - 4.0 * jnp.abs(fraction(degree + wave, 2.0))
            sign = jnp.where(southern, sign, 1.0)
            parts = split(table[slot])
            for third in range(THIRDS):
                pick = jnp.where(row == wanted + 16 * third, 1.0, 0.0).astype(jnp.bfloat16)
                for part, target in zip(parts, (table_high, table_low)):
                    placed = jnp.dot(part, pick, preferred_element_type=jnp.float32)
                    target[slot, third] = (placed * sign).astype(jnp.bfloat16)

    def transform(chunk):
        wait_circles(chunk)

        def cut(sector, _):
            values = circles[chunk, sector]
            values = jnp.concatenate([values, jnp.zeros((SECTOR_ROWS - 90, LANES), jnp.float32)], 0)
            high, low = split(values)
            rows = pl.ds(pl.multiple_of(sector * SECTOR_ROWS, SECTOR_ROWS), SECTOR_ROWS)
            points[rows, :LANES], points[rows, LANES:] = high, low
            return 0

        lax.fori_loop(0, SECTORS, cut, 0)

        def rows_of(part, _):
            rows = pl.ds(pl.multiple_of(part * 256, 256), 256)
            both = jnp.dot(matrix_high[rows, :], points[...], preferred_element_type=jnp.float32)
            rest = jnp.dot(matrix_low[rows, :], points[:, :LANES], preferred_element_type=jnp.float32)
            send_lat[chunk, rows, :] = both[:, :LANES] + both[:, LANES:] + rest
            return 0

        lax.fori_loop(0, 4, rows_of, 0)

    def turn_over(chunk):
        wait_blocks(1, recv_lat, chunk)

        def one(owner, _):
            for slot in range(2):
                for part in range(2):
                    values = recv_lat[chunk, pl.ds(part * 32 + owner * 2 + slot, 16, stride=BLOCK), :]
                    send_lon[chunk, pl.ds(pl.multiple_of(owner * BLOCK + slot * 32 + part * 16, 16), 16), :] = values
            return 0

        lax.fori_loop(0, SECTORS, one, 0)

    def sum_up(chunk):
        half, third = divmod(chunk, THIRDS)
        wait_blocks(2, recv_lon, chunk)
        arrived = recv_lon[chunk].reshape(16, 2, 2, 16, LANES)
        for slot in range(2):
            pair = [arrived[:, slot, part].reshape(256, LANES) for part in range(2)]
            high, low = split(jnp.concatenate(pair, 1))
            one_high, one_low = table_high[slot, third], table_low[slot, third]
            sums = jnp.dot(one_high, high, preferred_element_type=jnp.float32)
            sums += jnp.dot(one_high, low, preferred_element_type=jnp.float32)
            sums += jnp.dot(one_low, high, preferred_element_type=jnp.float32)
            for part in range(2):
                columns = pl.ds(part * 256 + half * LANES, LANES)
                piece = sums[:, part * LANES : (part + 1) * LANES]
                out[slot, :, columns] = out[slot, :, columns] + piece if third else piece

    def wait_sent(stage, source, chunk):
        if stage == 0:
            most = circles.at[chunk, pl.ds(0, SECTORS - 1)]
        else:
            most = source.at[chunk, pl.ds(0, 15 * BLOCK)]
        pltpu.make_async_copy(most, most, sems.at[2 * stage, chunk]).wait()

    load_rows(0).wait()
    pl.semaphore_wait(barrier, 30)
    burst(0)
    spread_waves()
    build_matrix()
    burst(1)
    transform(0)
    burst(2, 0)
    build_table()
    transform(1)
    burst(3, 1)
    turn_over(0)
    transform(2)
    burst(4, 2, 0)
    turn_over(1)
    transform(3)
    burst(5, 3, 1)
    turn_over(2)
    transform(4)
    burst(None, 4, 2)
    sum_up(0)
    turn_over(3)
    transform(5)
    burst(None, 5, 3)
    sum_up(1)
    turn_over(4)
    burst(None, None, 4)
    sum_up(2)
    sum_up(3)
    turn_over(5)
    burst(None, None, 5)
    sum_up(4)
    sum_up(5)
    for chunk in range(CHUNKS):
        wait_sent(0, None, chunk)
        wait_sent(1, send_lat, chunk)
        wait_sent(2, send_lon, chunk)


def on_device(grid_values, wave_table, legendre_basis):
    any_space = pl.BlockSpec(memory_space=pl.ANY)
    vmem = pl.BlockSpec(memory_space=pltpu.VMEM)
    return pl.pallas_call(
        kernel,
        out_shape=pltpu.VMEM((2, 720, 512), jnp.float32),
        in_specs=[any_space, vmem, any_space],
        out_specs=vmem,
        scratch_shapes=[
            pltpu.VMEM((CHUNKS, 90, 16, LANES), jnp.float32),
            pltpu.VMEM((CHUNKS, SECTORS, 90, LANES), jnp.float32),
            pltpu.VMEM((CHUNKS, SECTORS, 90, LANES), jnp.float32),
            pltpu.VMEM((512, LANES), jnp.float32),
            pltpu.VMEM((ALL_ROWS, POINTS), jnp.bfloat16),
            pltpu.VMEM((ALL_ROWS, POINTS), jnp.bfloat16),
            pltpu.VMEM((POINTS, 2 * LANES), jnp.bfloat16),
            pltpu.VMEM((CHUNKS, ALL_ROWS, LANES), jnp.float32),
            pltpu.VMEM((CHUNKS, ALL_ROWS, LANES), jnp.float32),
            pltpu.VMEM((CHUNKS, ALL_ROWS, LANES), jnp.float32),
            pltpu.VMEM((CHUNKS, ALL_ROWS, LANES), jnp.float32),
            pltpu.VMEM((2, 720, 384), jnp.float32),
            pltpu.VMEM((2, THIRDS, 720, 256), jnp.bfloat16),
            pltpu.VMEM((2, THIRDS, 720, 256), jnp.bfloat16),
            pltpu.SemaphoreType.DMA((6, CHUNKS)),
            pltpu.SemaphoreType.DMA((3, CHUNKS)),
            pltpu.SemaphoreType.DMA((CHUNKS,)),
            pltpu.SemaphoreType.DMA,
        ],
        compiler_params=pltpu.CompilerParams(
            collective_id=0, has_side_effects=True, vmem_limit_bytes=56 * 1024 * 1024
        ),
        name="transform",
    )(jnp.swapaxes(grid_values, 0, 1), wave_table.reshape(4, LANES), jnp.swapaxes(legendre_basis, 1, 2))


def solution(mesh):
    placed = (P("lat", "lon", None), P(), P(("lat", "lon"), None, None))
    return jax.shard_map(
        on_device,
        mesh=mesh,
        in_specs=placed,
        out_specs=P(("lat", "lon"), None, None),
        check_vma=False,
    )
```

```python
import functools
import math

import jax
import jax.numpy as jnp
from jax import lax
from jax.experimental import pallas as pl
from jax.experimental.pallas import tpu as pltpu
from jax.sharding import PartitionSpec as P

CIRCLE = 1440
LANES = 128
SECTORS = 16
BANDS = 16
SECTOR_ROWS = 96
POINTS = SECTORS * SECTOR_ROWS
THIRDS = 3
HALVES = 2
CHUNKS = THIRDS * HALVES
BLOCK = 64
ALL_ROWS = 16 * BLOCK


LON_STEPS = (
    (1, 0), (0, 1), (3, 0), (0, 3), (2, 1), (1, 2), (2, 3), (3, 2), (1, 1), (3, 3), (1, 3), (3, 1), (2, 0), (0, 2), (2, 2),
)
LAT_STEPS = (
    (1, 0), (7, 1), (2, 0), (6, 1), (3, 0), (5, 1), (4, 0), (4, 1), (7, 0), (1, 1), (6, 0), (2, 1), (5, 0), (3, 1), (0, 1),
)


def split(values):
    high = values.astype(jnp.bfloat16)
    low = (values - high.astype(jnp.float32)).astype(jnp.bfloat16)
    return high, low


def unit_circle(turns):
    half = turns * math.pi
    square = half * half
    sine = jnp.full_like(half, -1.0 / 39916800.0)
    for order in (9, 7, 5, 3, 1):
        sine = sine * square + (-1.0) ** (order // 2) / math.factorial(order)
    sine = sine * half
    cosine = jnp.full_like(half, 1.0 / 479001600.0)
    for order in (10, 8, 6, 4, 2, 0):
        cosine = cosine * square + (-1.0) ** (order // 2) / math.factorial(order)
    return 1.0 - 2.0 * sine * sine, 2.0 * sine * cosine


def fraction(product, circle):
    whole = jnp.floor(product * (1.0 / circle) + 0.5)
    return (product - whole * circle) * (1.0 / circle)


def kernel(
    grid, numbers, basis, out,
    rows_held, circles_out, circles, waves, matrix_high, matrix_low, points,
    send_lat, recv_lat, send_lon, recv_lon,
    table, table_high, table_low,
    sems, own_sems, row_sems, table_sem,
):
    lat = lax.axis_index("lat")
    lon = lax.axis_index("lon")
    northern = lat < 8
    place = jnp.where(northern, lat, 23 - lat)

    core = lax.rem(lat, 2)
    turn = 1 - 2 * core

    def lon_peer(step, way):
        x = lax.rem(lon // 4 + way * turn * step[0] + 4, 4)
        y = lax.rem(lax.rem(lon, 4) + way * turn * step[1] + 4, 4)
        return x * 4 + y

    def lat_peer(step):
        z = lax.rem(lat // 2 + turn * step[0] + 8, 8)
        return z * 2 + lax.rem(core + step[1], 2)

    def load_rows(chunk):
        half, third = divmod(chunk, THIRDS)
        first = pl.multiple_of(jnp.where(northern, 16 * third, 32 - 16 * third), 16)
        return pltpu.make_async_copy(
            grid.at[:, pl.ds(first, 16), pl.ds(half * LANES, LANES)], rows_held.at[chunk], row_sems.at[chunk]
        )

    for chunk in range(CHUNKS):
        load_rows(chunk).start()
    table_copy = pltpu.make_async_copy(basis, table, table_sem)
    table_copy.start()

    barrier = pltpu.get_barrier_semaphore()

    def greet(step, _):
        pl.semaphore_signal(barrier, inc=1, device_id={"lon": lax.rem(lon + step, SECTORS)}, device_id_type=pl.DeviceIdType.MESH)
        pl.semaphore_signal(barrier, inc=1, device_id={"lat": lax.rem(lat + step, BANDS)}, device_id_type=pl.DeviceIdType.MESH)
        return 0

    lax.fori_loop(1, 16, greet, 0)

    def arrange(chunk, owner):
        start = jnp.where(northern, owner, 15 - owner)
        circles_out[chunk, owner] = rows_held.at[chunk].reshape(90 * 16, LANES)[pl.ds(start, 90, stride=16), :]

    def send_circle(chunk, peer):
        if chunk:
            arrange(chunk, peer)
        pltpu.make_async_remote_copy(
            src_ref=circles_out.at[chunk, peer],
            dst_ref=circles.at[chunk, lon],
            send_sem=sems.at[0, chunk],
            recv_sem=sems.at[1, chunk],
            device_id={"lon": peer},
            device_id_type=pl.DeviceIdType.MESH,
        ).start()

    def keep_circle(chunk):
        if chunk:
            arrange(chunk, lon)
        pltpu.make_async_copy(circles_out.at[chunk, lon], circles.at[chunk, lon], own_sems.at[0, chunk]).start()

    def wait_circles(chunk):
        most = circles.at[chunk, pl.ds(0, SECTORS - 1)]
        pltpu.make_async_copy(most, most, sems.at[1, chunk]).wait()
        one = circles.at[chunk, 0]
        pltpu.make_async_copy(one, one, own_sems.at[0, chunk]).wait()

    def block_copy(stage, peer, chunk):
        source, target = ((send_lat, recv_lat), (send_lon, recv_lon))[stage - 1]
        mine = (place, lon)[stage - 1]
        return (
            source.at[chunk, pl.ds(pl.multiple_of(peer * BLOCK, BLOCK), BLOCK)],
            target.at[chunk, pl.ds(pl.multiple_of(mine * BLOCK, BLOCK), BLOCK)],
        )

    def send_block(stage, peer, chunk):
        source, target = block_copy(stage, peer, chunk)
        pltpu.make_async_remote_copy(
            src_ref=source,
            dst_ref=target,
            send_sem=sems.at[2 * stage, chunk],
            recv_sem=sems.at[2 * stage + 1, chunk],
            device_id={("lat", "lon")[stage - 1]: peer},
            device_id_type=pl.DeviceIdType.MESH,
        ).start()

    def keep_block(stage, chunk):
        source, target = block_copy(stage, (lat, lon)[stage - 1], chunk)
        pltpu.make_async_copy(source, target, own_sems.at[stage, chunk]).start()

    def circle_messages(chunk):
        return [functools.partial(lambda step: send_circle(chunk, lon_peer(step, 1)), step) for step in LON_STEPS]

    def lat_messages(chunk):
        return [functools.partial(lambda step: send_block(1, lat_peer(step), chunk), step) for step in LAT_STEPS]

    def lon_messages(chunk):
        return [functools.partial(lambda step: send_block(2, lon_peer(step, -1), chunk), step) for step in LON_STEPS]

    def burst(*lists):
        order = [((place + 0.5) / len(each), index, message) for index, each in enumerate(lists) for place, message in enumerate(each)]
        for _, _, message in sorted(order, key=lambda entry: entry[:2]):
            message()

    def wait_blocks(stage, target, chunk):
        most = target.at[chunk, pl.ds(0, 15 * BLOCK)]
        pltpu.make_async_copy(most, most, sems.at[2 * stage + 1, chunk]).wait()
        one = target.at[chunk, pl.ds(0, BLOCK)]
        pltpu.make_async_copy(one, one, own_sems.at[stage, chunk]).wait()

    def spread_waves():
        for group in range(4):
            values = jnp.broadcast_to(numbers[group : group + 1, :].astype(jnp.float32), (LANES, LANES))
            waves[LANES * group : LANES * (group + 1), :] = values.T

    def build_matrix():
        lane = lax.broadcasted_iota(jnp.int32, (32, LANES), 1).astype(jnp.float32)
        factor = 1.0 / math.sqrt(CIRCLE)

        def one(block, _):
            wave = waves[pl.ds(pl.multiple_of(block * 32, 32), 32), :]
            for group in range(3):
                position = lane + float(LANES * group)
                sector = jnp.floor(position * (1.0 / 96.0) + 0.001)
                point = position - 6.0 * sector
                cosine, sine = unit_circle(fraction(wave * point, float(CIRCLE)))
                cosine, sine = cosine * factor, sine * factor
                for quarter in range(4):
                    turn = fraction(wave * float(quarter), 4.0) * 4.0
                    turn_cos = 1.0 - jnp.abs(turn)
                    turn_sin = jnp.where(turn == -2.0, 0.0, turn)
                    real = turn_cos * cosine - turn_sin * sine
                    imaginary = -turn_sin * cosine - turn_cos * sine
                    columns = pl.ds(384 * quarter + LANES * group, LANES)
                    for offset, values in ((0, real), (32, imaginary)):
                        rows = pl.ds(pl.multiple_of(block * BLOCK + offset, 32), 32)
                        matrix_high[rows, columns], matrix_low[rows, columns] = split(values)
            return 0

        lax.fori_loop(0, 16, one, 0)

    def build_table():
        table_copy.wait()
        degree = lax.broadcasted_iota(jnp.int32, (720, 256), 0).astype(jnp.float32)
        row = lax.broadcasted_iota(jnp.int32, (384, 256), 0)
        column = lax.broadcasted_iota(jnp.int32, (384, 256), 1)
        wide_column = lax.broadcasted_iota(jnp.int32, (720, 256), 1)
        first = (lat * SECTORS + lon) * 2
        for slot in range(2):
            wave = jnp.broadcast_to(waves[pl.ds(first + slot, 1), :][:, :1], (1, 256))
            sign = 1.0 - 4.0 * jnp.abs(fraction(degree + wave, 2.0))
            parts = split(table[slot])
            for kind in range(THIRDS + 1):
                if kind < THIRDS:
                    wanted = 48 * (column & 7) + (column >> 4) + 16 * kind
                    southern = (wide_column & 8) == 8
                else:
                    wanted = 48 * ((column >> 4) & 7) + (column & 15) + 16 * (THIRDS - 1)
                    southern = wide_column >= 128
                pick = jnp.where(row == wanted, 1.0, 0.0).astype(jnp.bfloat16)
                signs = jnp.where(southern, sign, 1.0)
                for part, target in zip(parts, (table_high, table_low)):
                    placed = jnp.dot(part, pick, preferred_element_type=jnp.float32)
                    target[slot, kind] = (placed * signs).astype(jnp.bfloat16)

    def transform(chunk):
        wait_circles(chunk)

        def cut(sector, _):
            values = circles[chunk, sector]
            values = jnp.concatenate([values, jnp.zeros((SECTOR_ROWS - 90, LANES), jnp.float32)], 0)
            high, low = split(values)
            rows = pl.ds(pl.multiple_of(sector * SECTOR_ROWS, SECTOR_ROWS), SECTOR_ROWS)
            points[rows, :LANES], points[rows, LANES:] = high, low
            return 0

        lax.fori_loop(0, SECTORS, cut, 0)

        def rows_of(part):
            rows = pl.ds(pl.multiple_of(part * 256, 256), 256)
            both = jnp.dot(matrix_high[rows, :], points[...], preferred_element_type=jnp.float32)
            rest = jnp.dot(matrix_low[rows, :], points[:, :LANES], preferred_element_type=jnp.float32)
            send_lat[chunk, rows, :] = both[:, :LANES] + both[:, LANES:] + rest

        if chunk:
            lax.fori_loop(0, 4, lambda part, _: (rows_of(part), 0)[1], 0)
            return
        mine = lat // 4

        def one(step, _):
            part = lax.rem(mine + turn * (1 + 2 * step - 3 * (step // 2)) + 4, 4)
            rows_of(part)
            for number in range(4):
                send_block(1, part * 4 + lax.rem(lat + number, 4), 0)
            return 0

        lax.fori_loop(0, 3, one, 0)
        rows_of(mine)
        for number in range(1, 4):
            send_block(1, mine * 4 + lax.rem(lat + number, 4), 0)
        keep_block(1, 0)

    def regroup(chunk):
        def one(owner, _):
            for slot in range(2):
                values = send_lat[chunk, pl.ds(owner * 2 + slot, 32, stride=32), :]
                send_lon[chunk, pl.ds(pl.multiple_of(owner * BLOCK + slot * 32, 32), 32), :] = values
            return 0

        lax.fori_loop(0, SECTORS, one, 0)

    def turn_late(chunk):
        wait_blocks(2, recv_lon, chunk)

        def one(owner, _):
            for slot in range(2):
                for part in range(2):
                    values = recv_lon[chunk, pl.ds(slot * 32 + owner * 2 + part, 16, stride=BLOCK), :]
                    send_lat[chunk, pl.ds(pl.multiple_of(owner * BLOCK + slot * 32 + part * 16, 16), 16), :] = values
            return 0

        lax.fori_loop(0, BANDS, one, 0)

    def turn_over(chunk):
        wait_blocks(1, recv_lat, chunk)

        def one(owner, _):
            for slot in range(2):
                for part in range(2):
                    values = recv_lat[chunk, pl.ds(part * 32 + owner * 2 + slot, 16, stride=BLOCK), :]
                    send_lon[chunk, pl.ds(pl.multiple_of(owner * BLOCK + slot * 32 + part * 16, 16), 16), :] = values
            return 0

        lax.fori_loop(0, SECTORS, one, 0)

    def sum_up(chunk):
        half, third = divmod(chunk, THIRDS)
        late = chunk == CHUNKS - 1
        if late:
            wait_blocks(1, recv_lat, chunk)
        else:
            wait_blocks(2, recv_lon, chunk)
        arrived = (recv_lat if late else recv_lon)[chunk].reshape(16, 2, 2, 16, LANES)
        for slot in range(2):
            pair = [arrived[:, slot, part].reshape(256, LANES) for part in range(2)]
            high, low = split(jnp.concatenate(pair, 1))
            kind = THIRDS if late else third
            one_high, one_low = table_high[slot, kind], table_low[slot, kind]
            sums = jnp.dot(one_high, high, preferred_element_type=jnp.float32)
            sums += jnp.dot(one_high, low, preferred_element_type=jnp.float32)
            sums += jnp.dot(one_low, high, preferred_element_type=jnp.float32)
            for part in range(2):
                columns = pl.ds(part * 256 + half * LANES, LANES)
                piece = sums[:, part * LANES : (part + 1) * LANES]
                out[slot, :, columns] = out[slot, :, columns] + piece if third else piece

    def wait_sent(stage, source, chunk):
        if stage == 0:
            most = circles.at[chunk, pl.ds(0, SECTORS - 1)]
        else:
            most = source.at[chunk, pl.ds(0, 15 * BLOCK)]
        pltpu.make_async_copy(most, most, sems.at[2 * stage, chunk]).wait()

    load_rows(0).wait()
    lax.fori_loop(0, SECTORS, lambda owner, _: (arrange(0, owner), 0)[1], 0)
    pl.semaphore_wait(barrier, 30)
    burst(circle_messages(0))
    keep_circle(0)
    spread_waves()
    build_matrix()
    for chunk in range(1, CHUNKS):
        load_rows(chunk).wait()
    burst(circle_messages(1))
    keep_circle(1)
    transform(0)
    burst(circle_messages(2))
    keep_circle(2)
    build_table()
    transform(1)
    burst(lat_messages(1), circle_messages(3), circle_messages(4)[:8])
    keep_block(1, 1)
    keep_circle(3)
    transform(2)
    burst(lat_messages(2), circle_messages(4)[8:] + circle_messages(5))
    keep_block(1, 2)
    keep_circle(4)
    keep_circle(5)
    transform(3)
    turn_over(0)
    burst(lat_messages(3), lon_messages(0))
    keep_block(1, 3)
    keep_block(2, 0)
    transform(4)
    transform(5)
    regroup(5)
    burst(lon_messages(5))
    keep_block(2, 5)
    turn_over(1)
    turn_over(2)
    burst(lat_messages(4), lon_messages(1) + lon_messages(2))
    keep_block(1, 4)
    keep_block(2, 1)
    keep_block(2, 2)
    sum_up(0)
    turn_late(5)
    turn_over(3)
    burst(lat_messages(5), lon_messages(3))
    keep_block(1, 5)
    keep_block(2, 3)
    sum_up(1)
    sum_up(2)
    turn_over(4)
    burst(lon_messages(4))
    keep_block(2, 4)
    sum_up(3)
    sum_up(4)
    sum_up(5)
    for chunk in range(CHUNKS):
        wait_sent(0, None, chunk)
        wait_sent(1, send_lat, chunk)
        wait_sent(2, send_lon, chunk)


def on_device(grid_values, wave_table, legendre_basis):
    any_space = pl.BlockSpec(memory_space=pl.ANY)
    vmem = pl.BlockSpec(memory_space=pltpu.VMEM)
    return pl.pallas_call(
        kernel,
        out_shape=pltpu.VMEM((2, 720, 512), jnp.float32),
        in_specs=[any_space, vmem, any_space],
        out_specs=vmem,
        scratch_shapes=[
            pltpu.VMEM((CHUNKS, 90, 16, LANES), jnp.float32),
            pltpu.VMEM((CHUNKS, SECTORS, 90, LANES), jnp.float32),
            pltpu.VMEM((CHUNKS, SECTORS, 90, LANES), jnp.float32),
            pltpu.VMEM((512, LANES), jnp.float32),
            pltpu.VMEM((ALL_ROWS, POINTS), jnp.bfloat16),
            pltpu.VMEM((ALL_ROWS, POINTS), jnp.bfloat16),
            pltpu.VMEM((POINTS, 2 * LANES), jnp.bfloat16),
            pltpu.VMEM((CHUNKS, ALL_ROWS, LANES), jnp.float32),
            pltpu.VMEM((CHUNKS, ALL_ROWS, LANES), jnp.float32),
            pltpu.VMEM((CHUNKS, ALL_ROWS, LANES), jnp.float32),
            pltpu.VMEM((CHUNKS, ALL_ROWS, LANES), jnp.float32),
            pltpu.VMEM((2, 720, 384), jnp.float32),
            pltpu.VMEM((2, THIRDS + 1, 720, 256), jnp.bfloat16),
            pltpu.VMEM((2, THIRDS + 1, 720, 256), jnp.bfloat16),
            pltpu.SemaphoreType.DMA((6, CHUNKS)),
            pltpu.SemaphoreType.DMA((3, CHUNKS)),
            pltpu.SemaphoreType.DMA((CHUNKS,)),
            pltpu.SemaphoreType.DMA,
        ],
        compiler_params=pltpu.CompilerParams(
            collective_id=0, has_side_effects=True, vmem_limit_bytes=56 * 1024 * 1024
        ),
        name="transform",
    )(jnp.swapaxes(grid_values, 0, 1), wave_table.reshape(4, LANES), jnp.swapaxes(legendre_basis, 1, 2))


def solution(mesh):
    placed = (P("lat", "lon", None), P(), P(("lat", "lon"), None, None))
    return jax.shard_map(
        on_device,
        mesh=mesh,
        in_specs=placed,
        out_specs=P(("lat", "lon"), None, None),
        check_vma=False,
    )
```

```python
import functools
import math

import jax
import jax.numpy as jnp
from jax import lax
from jax.experimental import pallas as pl
from jax.experimental.pallas import tpu as pltpu
from jax.sharding import PartitionSpec as P

CIRCLE = 1440
LANES = 128
SECTORS = 16
BANDS = 16
SECTOR_ROWS = 96
POINTS = SECTORS * SECTOR_ROWS
THIRDS = 3
HALVES = 2
CHUNKS = THIRDS * HALVES
BLOCK = 64
ALL_ROWS = 16 * BLOCK


LON_STEPS = (
    (2, 2), (2, 1), (1, 2), (2, 3), (3, 2), (1, 1), (3, 3), (1, 3), (3, 1), (2, 0), (0, 2), (1, 0), (0, 1), (3, 0), (0, 3),
)
FAR_LAT_STEPS = (
    (4, 0), (4, 1), (3, 0), (5, 1), (3, 1), (5, 0), (2, 0), (6, 1), (2, 1), (6, 0), (1, 0), (7, 1), (1, 1), (7, 0), (0, 1),
)
LAT_STEPS = (
    (1, 0), (7, 1), (2, 0), (6, 1), (3, 0), (5, 1), (4, 0), (4, 1), (7, 0), (1, 1), (6, 0), (2, 1), (5, 0), (3, 1), (0, 1),
)


def split(values):
    high = values.astype(jnp.bfloat16)
    low = (values - high.astype(jnp.float32)).astype(jnp.bfloat16)
    return high, low


def unit_circle(turns):
    half = turns * math.pi
    square = half * half
    sine = jnp.full_like(half, -1.0 / 39916800.0)
    for order in (9, 7, 5, 3, 1):
        sine = sine * square + (-1.0) ** (order // 2) / math.factorial(order)
    sine = sine * half
    cosine = jnp.full_like(half, 1.0 / 479001600.0)
    for order in (10, 8, 6, 4, 2, 0):
        cosine = cosine * square + (-1.0) ** (order // 2) / math.factorial(order)
    return 1.0 - 2.0 * sine * sine, 2.0 * sine * cosine


def fraction(product, circle):
    whole = jnp.floor(product * (1.0 / circle) + 0.5)
    return (product - whole * circle) * (1.0 / circle)


def kernel(
    grid, numbers, basis, out,
    rows_held, circles_out, circles, waves, matrix_high, matrix_low, points,
    send_lat, recv_lat, send_lon, recv_lon,
    table, table_high, table_low,
    sems, own_sems, row_sems, table_sem,
):
    lat = lax.axis_index("lat")
    lon = lax.axis_index("lon")
    northern = lat < 8
    place = jnp.where(northern, lat, 23 - lat)

    core = lax.rem(lat, 2)
    turn = 1 - 2 * core

    def lon_peer(step, way):
        x = lax.rem(lon // 4 + way * turn * step[0] + 4, 4)
        y = lax.rem(lax.rem(lon, 4) + way * turn * step[1] + 4, 4)
        return x * 4 + y

    def lat_peer(step):
        z = lax.rem(lat // 2 + turn * step[0] + 8, 8)
        return z * 2 + lax.rem(core + step[1], 2)

    def load_rows(chunk):
        half, third = divmod(chunk, THIRDS)
        first = pl.multiple_of(jnp.where(northern, 16 * third, 32 - 16 * third), 16)
        return pltpu.make_async_copy(
            grid.at[:, pl.ds(first, 16), pl.ds(half * LANES, LANES)], rows_held.at[chunk], row_sems.at[chunk]
        )

    for chunk in range(CHUNKS):
        load_rows(chunk).start()
    table_copy = pltpu.make_async_copy(basis, table, table_sem)
    table_copy.start()

    barrier = pltpu.get_barrier_semaphore()

    for step in LON_STEPS:
        pl.semaphore_signal(barrier, inc=1, device_id={"lon": lon_peer(step, 1)}, device_id_type=pl.DeviceIdType.MESH)
    for step in FAR_LAT_STEPS:
        pl.semaphore_signal(barrier, inc=1, device_id={"lat": lat_peer(step)}, device_id_type=pl.DeviceIdType.MESH)

    def arrange(chunk, owner):
        start = jnp.where(northern, owner, 15 - owner)
        circles_out[chunk, owner] = rows_held.at[chunk].reshape(90 * 16, LANES)[pl.ds(start, 90, stride=16), :]

    def send_circle(chunk, peer):
        if chunk:
            arrange(chunk, peer)
        pltpu.make_async_remote_copy(
            src_ref=circles_out.at[chunk, peer],
            dst_ref=circles.at[chunk, lon],
            send_sem=sems.at[0, chunk],
            recv_sem=sems.at[1, chunk],
            device_id={"lon": peer},
            device_id_type=pl.DeviceIdType.MESH,
        ).start()

    def keep_circle(chunk):
        if chunk:
            arrange(chunk, lon)
        pltpu.make_async_copy(circles_out.at[chunk, lon], circles.at[chunk, lon], own_sems.at[0, chunk]).start()

    def wait_circles(chunk):
        most = circles.at[chunk, pl.ds(0, SECTORS - 1)]
        pltpu.make_async_copy(most, most, sems.at[1, chunk]).wait()
        one = circles.at[chunk, 0]
        pltpu.make_async_copy(one, one, own_sems.at[0, chunk]).wait()

    def block_copy(stage, peer, chunk):
        source, target = ((send_lat, recv_lat), (send_lon, recv_lon))[stage - 1]
        mine = (place, lon)[stage - 1]
        return (
            source.at[chunk, pl.ds(pl.multiple_of(peer * BLOCK, BLOCK), BLOCK)],
            target.at[chunk, pl.ds(pl.multiple_of(mine * BLOCK, BLOCK), BLOCK)],
        )

    def send_block(stage, peer, chunk):
        source, target = block_copy(stage, peer, chunk)
        pltpu.make_async_remote_copy(
            src_ref=source,
            dst_ref=target,
            send_sem=sems.at[2 * stage, chunk],
            recv_sem=sems.at[2 * stage + 1, chunk],
            device_id={("lat", "lon")[stage - 1]: peer},
            device_id_type=pl.DeviceIdType.MESH,
        ).start()

    def keep_block(stage, chunk):
        source, target = block_copy(stage, (lat, lon)[stage - 1], chunk)
        pltpu.make_async_copy(source, target, own_sems.at[stage, chunk]).start()

    def circle_messages(chunk):
        return [functools.partial(lambda step: send_circle(chunk, lon_peer(step, 1)), step) for step in LON_STEPS]

    def lat_messages(chunk):
        return [functools.partial(lambda step: send_block(1, lat_peer(step), chunk), step) for step in LAT_STEPS]

    def lon_messages(chunk):
        return [functools.partial(lambda step: send_block(2, lon_peer(step, -1), chunk), step) for step in LON_STEPS]

    def burst(*lists):
        order = [((place + 0.5) / len(each), index, message) for index, each in enumerate(lists) for place, message in enumerate(each)]
        for _, _, message in sorted(order, key=lambda entry: entry[:2]):
            message()

    def wait_blocks(stage, target, chunk):
        most = target.at[chunk, pl.ds(0, 15 * BLOCK)]
        pltpu.make_async_copy(most, most, sems.at[2 * stage + 1, chunk]).wait()
        one = target.at[chunk, pl.ds(0, BLOCK)]
        pltpu.make_async_copy(one, one, own_sems.at[stage, chunk]).wait()

    def spread_waves():
        for group in range(4):
            values = jnp.broadcast_to(numbers[group : group + 1, :].astype(jnp.float32), (LANES, LANES))
            waves[LANES * group : LANES * (group + 1), :] = values.T

    def build_matrix():
        lane = lax.broadcasted_iota(jnp.int32, (32, LANES), 1).astype(jnp.float32)
        factor = 1.0 / math.sqrt(CIRCLE)

        def one(block, _):
            wave = waves[pl.ds(pl.multiple_of(block * 32, 32), 32), :]
            for group in range(3):
                position = lane + float(LANES * group)
                sector = jnp.floor(position * (1.0 / 96.0) + 0.001)
                point = position - 6.0 * sector
                cosine, sine = unit_circle(fraction(wave * point, float(CIRCLE)))
                cosine, sine = cosine * factor, sine * factor
                for quarter in range(4):
                    turn = fraction(wave * float(quarter), 4.0) * 4.0
                    turn_cos = 1.0 - jnp.abs(turn)
                    turn_sin = jnp.where(turn == -2.0, 0.0, turn)
                    real = turn_cos * cosine - turn_sin * sine
                    imaginary = -turn_sin * cosine - turn_cos * sine
                    columns = pl.ds(384 * quarter + LANES * group, LANES)
                    for offset, values in ((0, real), (32, imaginary)):
                        rows = pl.ds(pl.multiple_of(block * BLOCK + offset, 32), 32)
                        matrix_high[rows, columns], matrix_low[rows, columns] = split(values)
            return 0

        lax.fori_loop(0, 16, one, 0)

    def build_table():
        table_copy.wait()
        degree = lax.broadcasted_iota(jnp.int32, (720, 256), 0).astype(jnp.float32)
        row = lax.broadcasted_iota(jnp.int32, (384, 256), 0)
        column = lax.broadcasted_iota(jnp.int32, (384, 256), 1)
        wide_column = lax.broadcasted_iota(jnp.int32, (720, 256), 1)
        first = (lat * SECTORS + lon) * 2
        for slot in range(2):
            wave = jnp.broadcast_to(waves[pl.ds(first + slot, 1), :][:, :1], (1, 256))
            sign = 1.0 - 4.0 * jnp.abs(fraction(degree + wave, 2.0))
            parts = split(table[slot])
            for kind in range(THIRDS + 1):
                if kind < THIRDS:
                    wanted = 48 * (column & 7) + (column >> 4) + 16 * kind
                    southern = (wide_column & 8) == 8
                else:
                    wanted = 48 * ((column >> 4) & 7) + (column & 15) + 16 * (THIRDS - 1)
                    southern = wide_column >= 128
                pick = jnp.where(row == wanted, 1.0, 0.0).astype(jnp.bfloat16)
                signs = jnp.where(southern, sign, 1.0)
                for part, target in zip(parts, (table_high, table_low)):
                    placed = jnp.dot(part, pick, preferred_element_type=jnp.float32)
                    target[slot, kind] = (placed * signs).astype(jnp.bfloat16)

    def transform(chunk):
        wait_circles(chunk)

        def cut(sector, _):
            values = circles[chunk, sector]
            values = jnp.concatenate([values, jnp.zeros((SECTOR_ROWS - 90, LANES), jnp.float32)], 0)
            high, low = split(values)
            rows = pl.ds(pl.multiple_of(sector * SECTOR_ROWS, SECTOR_ROWS), SECTOR_ROWS)
            points[rows, :LANES], points[rows, LANES:] = high, low
            return 0

        lax.fori_loop(0, SECTORS, cut, 0)

        def rows_of(part):
            rows = pl.ds(pl.multiple_of(part * 256, 256), 256)
            both = jnp.dot(matrix_high[rows, :], points[...], preferred_element_type=jnp.float32)
            rest = jnp.dot(matrix_low[rows, :], points[:, :LANES], preferred_element_type=jnp.float32)
            send_lat[chunk, rows, :] = both[:, :LANES] + both[:, LANES:] + rest

        if chunk:
            lax.fori_loop(0, 4, lambda part, _: (rows_of(part), 0)[1], 0)
            return
        mine = lat // 4

        def one(step, _):
            part = lax.rem(mine + turn * (1 + 2 * step - 3 * (step // 2)) + 4, 4)
            rows_of(part)
            for number in range(4):
                send_block(1, part * 4 + lax.rem(lat + number, 4), 0)
            return 0

        lax.fori_loop(0, 3, one, 0)
        rows_of(mine)
        for number in range(1, 4):
            send_block(1, mine * 4 + lax.rem(lat + number, 4), 0)
        keep_block(1, 0)

    def regroup(chunk):
        def one(owner, _):
            for slot in range(2):
                values = send_lat[chunk, pl.ds(owner * 2 + slot, 32, stride=32), :]
                send_lon[chunk, pl.ds(pl.multiple_of(owner * BLOCK + slot * 32, 32), 32), :] = values
            return 0

        lax.fori_loop(0, SECTORS, one, 0)

    def turn_late(chunk):
        wait_blocks(2, recv_lon, chunk)

        def one(owner, _):
            for slot in range(2):
                for part in range(2):
                    values = recv_lon[chunk, pl.ds(slot * 32 + owner * 2 + part, 16, stride=BLOCK), :]
                    send_lat[chunk, pl.ds(pl.multiple_of(owner * BLOCK + slot * 32 + part * 16, 16), 16), :] = values
            return 0

        lax.fori_loop(0, BANDS, one, 0)

    def turn_over(chunk):
        wait_blocks(1, recv_lat, chunk)

        def one(owner, _):
            for slot in range(2):
                for part in range(2):
                    values = recv_lat[chunk, pl.ds(part * 32 + owner * 2 + slot, 16, stride=BLOCK), :]
                    send_lon[chunk, pl.ds(pl.multiple_of(owner * BLOCK + slot * 32 + part * 16, 16), 16), :] = values
            return 0

        lax.fori_loop(0, SECTORS, one, 0)

    def sum_up(chunk):
        half, third = divmod(chunk, THIRDS)
        late = chunk == CHUNKS - 1
        if late:
            wait_blocks(1, recv_lat, chunk)
        else:
            wait_blocks(2, recv_lon, chunk)
        arrived = (recv_lat if late else recv_lon)[chunk].reshape(16, 2, 2, 16, LANES)
        for slot in range(2):
            pair = [arrived[:, slot, part].reshape(256, LANES) for part in range(2)]
            high, low = split(jnp.concatenate(pair, 1))
            kind = THIRDS if late else third
            one_high, one_low = table_high[slot, kind], table_low[slot, kind]
            sums = jnp.dot(one_high, high, preferred_element_type=jnp.float32)
            sums += jnp.dot(one_high, low, preferred_element_type=jnp.float32)
            sums += jnp.dot(one_low, high, preferred_element_type=jnp.float32)
            for part in range(2):
                columns = pl.ds(part * 256 + half * LANES, LANES)
                piece = sums[:, part * LANES : (part + 1) * LANES]
                out[slot, :, columns] = out[slot, :, columns] + piece if third else piece

    def wait_sent(stage, source, chunk):
        if stage == 0:
            most = circles.at[chunk, pl.ds(0, SECTORS - 1)]
        else:
            most = source.at[chunk, pl.ds(0, 15 * BLOCK)]
        pltpu.make_async_copy(most, most, sems.at[2 * stage, chunk]).wait()

    load_rows(0).wait()
    lax.fori_loop(0, SECTORS, lambda owner, _: (arrange(0, owner), 0)[1], 0)
    pl.semaphore_wait(barrier, 30)
    burst(circle_messages(0))
    keep_circle(0)
    spread_waves()
    build_matrix()
    for chunk in range(1, CHUNKS):
        load_rows(chunk).wait()
    burst(circle_messages(1))
    keep_circle(1)
    transform(0)
    burst(circle_messages(2))
    keep_circle(2)
    build_table()
    transform(1)
    burst(lat_messages(1), circle_messages(3), circle_messages(4)[:8])
    keep_block(1, 1)
    keep_circle(3)
    transform(2)
    burst(lat_messages(2), circle_messages(4)[8:] + circle_messages(5))
    keep_block(1, 2)
    keep_circle(4)
    keep_circle(5)
    transform(3)
    turn_over(0)
    burst(lat_messages(3), lon_messages(0))
    keep_block(1, 3)
    keep_block(2, 0)
    transform(4)
    transform(5)
    regroup(5)
    burst(lon_messages(5))
    keep_block(2, 5)
    turn_over(1)
    turn_over(2)
    burst(lat_messages(4), lon_messages(1) + lon_messages(2))
    keep_block(1, 4)
    keep_block(2, 1)
    keep_block(2, 2)
    sum_up(0)
    turn_late(5)
    turn_over(3)
    burst(lat_messages(5), lon_messages(3))
    keep_block(1, 5)
    keep_block(2, 3)
    sum_up(1)
    sum_up(2)
    turn_over(4)
    burst(lon_messages(4))
    keep_block(2, 4)
    sum_up(3)
    sum_up(5)
    sum_up(4)
    for chunk in range(CHUNKS):
        wait_sent(0, None, chunk)
        wait_sent(1, send_lat, chunk)
        wait_sent(2, send_lon, chunk)


def on_device(grid_values, wave_table, legendre_basis):
    any_space = pl.BlockSpec(memory_space=pl.ANY)
    vmem = pl.BlockSpec(memory_space=pltpu.VMEM)
    return pl.pallas_call(
        kernel,
        out_shape=pltpu.VMEM((2, 720, 512), jnp.float32),
        in_specs=[any_space, vmem, any_space],
        out_specs=vmem,
        scratch_shapes=[
            pltpu.VMEM((CHUNKS, 90, 16, LANES), jnp.float32),
            pltpu.VMEM((CHUNKS, SECTORS, 90, LANES), jnp.float32),
            pltpu.VMEM((CHUNKS, SECTORS, 90, LANES), jnp.float32),
            pltpu.VMEM((512, LANES), jnp.float32),
            pltpu.VMEM((ALL_ROWS, POINTS), jnp.bfloat16),
            pltpu.VMEM((ALL_ROWS, POINTS), jnp.bfloat16),
            pltpu.VMEM((POINTS, 2 * LANES), jnp.bfloat16),
            pltpu.VMEM((CHUNKS, ALL_ROWS, LANES), jnp.float32),
            pltpu.VMEM((CHUNKS, ALL_ROWS, LANES), jnp.float32),
            pltpu.VMEM((CHUNKS, ALL_ROWS, LANES), jnp.float32),
            pltpu.VMEM((CHUNKS, ALL_ROWS, LANES), jnp.float32),
            pltpu.VMEM((2, 720, 384), jnp.float32),
            pltpu.VMEM((2, THIRDS + 1, 720, 256), jnp.bfloat16),
            pltpu.VMEM((2, THIRDS + 1, 720, 256), jnp.bfloat16),
            pltpu.SemaphoreType.DMA((6, CHUNKS)),
            pltpu.SemaphoreType.DMA((3, CHUNKS)),
            pltpu.SemaphoreType.DMA((CHUNKS,)),
            pltpu.SemaphoreType.DMA,
        ],
        compiler_params=pltpu.CompilerParams(
            collective_id=0, has_side_effects=True, vmem_limit_bytes=56 * 1024 * 1024
        ),
        name="transform",
    )(jnp.swapaxes(grid_values, 0, 1), wave_table.reshape(4, LANES), jnp.swapaxes(legendre_basis, 1, 2))


def solution(mesh):
    placed = (P("lat", "lon", None), P(), P(("lat", "lon"), None, None))
    return jax.shard_map(
        on_device,
        mesh=mesh,
        in_specs=placed,
        out_specs=P(("lat", "lon"), None, None),
        check_vma=False,
    )
```

```python
import functools
import math

import jax
import jax.numpy as jnp
from jax import lax
from jax.experimental import pallas as pl
from jax.experimental.pallas import tpu as pltpu
from jax.sharding import PartitionSpec as P

CIRCLE = 1440
LANES = 128
SECTORS = 16
BANDS = 16
SECTOR_ROWS = 96
POINTS = SECTORS * SECTOR_ROWS
THIRDS = 3
HALVES = 2
CHUNKS = THIRDS * HALVES
BLOCK = 64
ALL_ROWS = 16 * BLOCK


LON_STEPS = (
    (2, 2), (2, 1), (1, 2), (2, 3), (3, 2), (1, 1), (3, 3), (1, 3), (3, 1), (2, 0), (0, 2), (1, 0), (0, 1), (3, 0), (0, 3),
)
FAR_LAT_STEPS = (
    (4, 0), (4, 1), (3, 0), (5, 1), (3, 1), (5, 0), (2, 0), (6, 1), (2, 1), (6, 0), (1, 0), (7, 1), (1, 1), (7, 0), (0, 1),
)
LAT_STEPS = (
    (1, 0), (7, 1), (2, 0), (6, 1), (3, 0), (5, 1), (4, 0), (4, 1), (7, 0), (1, 1), (6, 0), (2, 1), (5, 0), (3, 1), (0, 1),
)


def split(values):
    high = values.astype(jnp.bfloat16)
    low = (values - high.astype(jnp.float32)).astype(jnp.bfloat16)
    return high, low


def unit_circle(turns):
    half = turns * math.pi
    square = half * half
    sine = jnp.full_like(half, -1.0 / 39916800.0)
    for order in (9, 7, 5, 3, 1):
        sine = sine * square + (-1.0) ** (order // 2) / math.factorial(order)
    sine = sine * half
    cosine = jnp.full_like(half, 1.0 / 479001600.0)
    for order in (10, 8, 6, 4, 2, 0):
        cosine = cosine * square + (-1.0) ** (order // 2) / math.factorial(order)
    return 1.0 - 2.0 * sine * sine, 2.0 * sine * cosine


def fraction(product, circle):
    whole = jnp.floor(product * (1.0 / circle) + 0.5)
    return (product - whole * circle) * (1.0 / circle)


def kernel(
    grid, numbers, basis, out,
    rows_held, circles_out, circles, waves, matrix_high, matrix_low, points,
    send_lat, recv_lat, send_lon, recv_lon,
    table, table_high, table_low,
    sems, own_sems, row_sems, table_sem,
):
    lat = lax.axis_index("lat")
    lon = lax.axis_index("lon")
    northern = lat < 8
    place = jnp.where(northern, lat, 23 - lat)

    core = lax.rem(lat, 2)
    turn = 1 - 2 * core

    def lon_peer(step, way):
        x = lax.rem(lon // 4 + way * turn * step[0] + 4, 4)
        y = lax.rem(lax.rem(lon, 4) + way * turn * step[1] + 4, 4)
        return x * 4 + y

    def lat_peer(step):
        z = lax.rem(lat // 2 + turn * step[0] + 8, 8)
        return z * 2 + lax.rem(core + step[1], 2)

    def load_rows(chunk):
        half, third = divmod(chunk, THIRDS)
        first = pl.multiple_of(jnp.where(northern, 16 * third, 32 - 16 * third), 16)
        return pltpu.make_async_copy(
            grid.at[:, pl.ds(first, 16), pl.ds(half * LANES, LANES)], rows_held.at[chunk], row_sems.at[chunk]
        )

    load_rows(0).start()
    barrier = pltpu.get_barrier_semaphore()
    for lat_step, lon_step in zip(FAR_LAT_STEPS, LON_STEPS):
        pl.semaphore_signal(barrier, inc=1, device_id={"lat": lat_peer(lat_step)}, device_id_type=pl.DeviceIdType.MESH)
        pl.semaphore_signal(barrier, inc=1, device_id={"lon": lon_peer(lon_step, 1)}, device_id_type=pl.DeviceIdType.MESH)
    for chunk in range(1, CHUNKS):
        load_rows(chunk).start()
    table_copy = pltpu.make_async_copy(basis, table, table_sem)
    table_copy.start()

    def arrange(chunk, owner):
        start = jnp.where(northern, owner, 15 - owner)
        circles_out[chunk, owner] = rows_held.at[chunk].reshape(90 * 16, LANES)[pl.ds(start, 90, stride=16), :]

    def send_circle(chunk, peer):
        if chunk:
            arrange(chunk, peer)
        pltpu.make_async_remote_copy(
            src_ref=circles_out.at[chunk, peer],
            dst_ref=circles.at[chunk, lon],
            send_sem=sems.at[0, chunk],
            recv_sem=sems.at[1, chunk],
            device_id={"lon": peer},
            device_id_type=pl.DeviceIdType.MESH,
        ).start()

    def keep_circle(chunk):
        if chunk:
            arrange(chunk, lon)
        pltpu.make_async_copy(circles_out.at[chunk, lon], circles.at[chunk, lon], own_sems.at[0, chunk]).start()

    def wait_circles(chunk):
        most = circles.at[chunk, pl.ds(0, SECTORS - 1)]
        pltpu.make_async_copy(most, most, sems.at[1, chunk]).wait()
        one = circles.at[chunk, 0]
        pltpu.make_async_copy(one, one, own_sems.at[0, chunk]).wait()

    def block_copy(stage, peer, chunk):
        source, target = ((send_lat, recv_lat), (send_lon, recv_lon))[stage - 1]
        mine = (place, lon)[stage - 1]
        return (
            source.at[chunk, pl.ds(pl.multiple_of(peer * BLOCK, BLOCK), BLOCK)],
            target.at[chunk, pl.ds(pl.multiple_of(mine * BLOCK, BLOCK), BLOCK)],
        )

    def send_block(stage, peer, chunk):
        source, target = block_copy(stage, peer, chunk)
        pltpu.make_async_remote_copy(
            src_ref=source,
            dst_ref=target,
            send_sem=sems.at[2 * stage, chunk],
            recv_sem=sems.at[2 * stage + 1, chunk],
            device_id={("lat", "lon")[stage - 1]: peer},
            device_id_type=pl.DeviceIdType.MESH,
        ).start()

    def keep_block(stage, chunk):
        source, target = block_copy(stage, (lat, lon)[stage - 1], chunk)
        pltpu.make_async_copy(source, target, own_sems.at[stage, chunk]).start()

    def circle_messages(chunk):
        return [functools.partial(lambda step: send_circle(chunk, lon_peer(step, 1)), step) for step in LON_STEPS]

    def lat_messages(chunk):
        return [functools.partial(lambda step: send_block(1, lat_peer(step), chunk), step) for step in LAT_STEPS]

    def lon_messages(chunk):
        return [functools.partial(lambda step: send_block(2, lon_peer(step, -1), chunk), step) for step in LON_STEPS]

    def burst(*lists):
        order = [((place + 0.5) / len(each), index, message) for index, each in enumerate(lists) for place, message in enumerate(each)]
        for _, _, message in sorted(order, key=lambda entry: entry[:2]):
            message()

    def wait_blocks(stage, target, chunk):
        most = target.at[chunk, pl.ds(0, 15 * BLOCK)]
        pltpu.make_async_copy(most, most, sems.at[2 * stage + 1, chunk]).wait()
        one = target.at[chunk, pl.ds(0, BLOCK)]
        pltpu.make_async_copy(one, one, own_sems.at[stage, chunk]).wait()

    def spread_waves():
        for group in range(4):
            values = jnp.broadcast_to(numbers[group : group + 1, :].astype(jnp.float32), (LANES, LANES))
            waves[LANES * group : LANES * (group + 1), :] = values.T

    def build_matrix():
        lane = lax.broadcasted_iota(jnp.int32, (32, LANES), 1).astype(jnp.float32)
        factor = 1.0 / math.sqrt(CIRCLE)

        def one(block, _):
            wave = waves[pl.ds(pl.multiple_of(block * 32, 32), 32), :]
            for group in range(3):
                position = lane + float(LANES * group)
                sector = jnp.floor(position * (1.0 / 96.0) + 0.001)
                point = position - 6.0 * sector
                cosine, sine = unit_circle(fraction(wave * point, float(CIRCLE)))
                cosine, sine = cosine * factor, sine * factor
                for quarter in range(4):
                    turn = fraction(wave * float(quarter), 4.0) * 4.0
                    turn_cos = 1.0 - jnp.abs(turn)
                    turn_sin = jnp.where(turn == -2.0, 0.0, turn)
                    real = turn_cos * cosine - turn_sin * sine
                    imaginary = -turn_sin * cosine - turn_cos * sine
                    columns = pl.ds(384 * quarter + LANES * group, LANES)
                    for offset, values in ((0, real), (32, imaginary)):
                        rows = pl.ds(pl.multiple_of(block * BLOCK + offset, 32), 32)
                        matrix_high[rows, columns], matrix_low[rows, columns] = split(values)
            return 0

        lax.fori_loop(0, 16, one, 0)

    def build_table():
        table_copy.wait()
        degree = lax.broadcasted_iota(jnp.int32, (720, 256), 0).astype(jnp.float32)
        row = lax.broadcasted_iota(jnp.int32, (384, 256), 0)
        column = lax.broadcasted_iota(jnp.int32, (384, 256), 1)
        wide_column = lax.broadcasted_iota(jnp.int32, (720, 256), 1)
        first = (lat * SECTORS + lon) * 2
        for slot in range(2):
            wave = jnp.broadcast_to(waves[pl.ds(first + slot, 1), :][:, :1], (1, 256))
            sign = 1.0 - 4.0 * jnp.abs(fraction(degree + wave, 2.0))
            parts = split(table[slot])
            for kind in range(THIRDS + 1):
                if kind < THIRDS:
                    wanted = 48 * (column & 7) + (column >> 4) + 16 * kind
                    southern = (wide_column & 8) == 8
                else:
                    wanted = 48 * ((column >> 4) & 7) + (column & 15) + 16 * (THIRDS - 1)
                    southern = wide_column >= 128
                pick = jnp.where(row == wanted, 1.0, 0.0).astype(jnp.bfloat16)
                signs = jnp.where(southern, sign, 1.0)
                for part, target in zip(parts, (table_high, table_low)):
                    placed = jnp.dot(part, pick, preferred_element_type=jnp.float32)
                    target[slot, kind] = (placed * signs).astype(jnp.bfloat16)

    def transform(chunk):
        wait_circles(chunk)

        def cut(sector, _):
            values = circles[chunk, sector]
            values = jnp.concatenate([values, jnp.zeros((SECTOR_ROWS - 90, LANES), jnp.float32)], 0)
            high, low = split(values)
            rows = pl.ds(pl.multiple_of(sector * SECTOR_ROWS, SECTOR_ROWS), SECTOR_ROWS)
            points[rows, :LANES], points[rows, LANES:] = high, low
            return 0

        lax.fori_loop(0, SECTORS, cut, 0)

        def rows_of(part):
            rows = pl.ds(pl.multiple_of(part * 256, 256), 256)
            both = jnp.dot(matrix_high[rows, :], points[...], preferred_element_type=jnp.float32)
            rest = jnp.dot(matrix_low[rows, :], points[:, :LANES], preferred_element_type=jnp.float32)
            send_lat[chunk, rows, :] = both[:, :LANES] + both[:, LANES:] + rest

        if chunk:
            lax.fori_loop(0, 4, lambda part, _: (rows_of(part), 0)[1], 0)
            return
        mine = lat // 4

        def one(step, _):
            part = lax.rem(mine + turn * (1 + 2 * step - 3 * (step // 2)) + 4, 4)
            rows_of(part)
            for number in range(4):
                send_block(1, part * 4 + lax.rem(lat + number, 4), 0)
            return 0

        lax.fori_loop(0, 3, one, 0)
        rows_of(mine)
        for number in range(1, 4):
            send_block(1, mine * 4 + lax.rem(lat + number, 4), 0)
        keep_block(1, 0)

    def regroup(chunk):
        def one(owner, _):
            for slot in range(2):
                values = send_lat[chunk, pl.ds(owner * 2 + slot, 32, stride=32), :]
                send_lon[chunk, pl.ds(pl.multiple_of(owner * BLOCK + slot * 32, 32), 32), :] = values
            return 0

        lax.fori_loop(0, SECTORS, one, 0)

    def turn_late(chunk):
        wait_blocks(2, recv_lon, chunk)

        def one(owner, _):
            for slot in range(2):
                for part in range(2):
                    values = recv_lon[chunk, pl.ds(slot * 32 + owner * 2 + part, 16, stride=BLOCK), :]
                    send_lat[chunk, pl.ds(pl.multiple_of(owner * BLOCK + slot * 32 + part * 16, 16), 16), :] = values
            return 0

        lax.fori_loop(0, BANDS, one, 0)

    def turn_over(chunk):
        wait_blocks(1, recv_lat, chunk)

        def one(owner, _):
            for slot in range(2):
                for part in range(2):
                    values = recv_lat[chunk, pl.ds(part * 32 + owner * 2 + slot, 16, stride=BLOCK), :]
                    send_lon[chunk, pl.ds(pl.multiple_of(owner * BLOCK + slot * 32 + part * 16, 16), 16), :] = values
            return 0

        lax.fori_loop(0, SECTORS, one, 0)

    def sum_up(chunk):
        half, third = divmod(chunk, THIRDS)
        late = chunk == CHUNKS - 1
        if late:
            wait_blocks(1, recv_lat, chunk)
        else:
            wait_blocks(2, recv_lon, chunk)
        arrived = (recv_lat if late else recv_lon)[chunk].reshape(16, 2, 2, 16, LANES)
        for slot in range(2):
            pair = [arrived[:, slot, part].reshape(256, LANES) for part in range(2)]
            high, low = split(jnp.concatenate(pair, 1))
            kind = THIRDS if late else third
            one_high, one_low = table_high[slot, kind], table_low[slot, kind]
            sums = jnp.dot(
                jnp.concatenate([one_high, one_high, one_low], 1),
                jnp.concatenate([high, low, high], 0),
                preferred_element_type=jnp.float32,
            )
            for part in range(2):
                columns = pl.ds(part * 256 + half * LANES, LANES)
                piece = sums[:, part * LANES : (part + 1) * LANES]
                out[slot, :, columns] = out[slot, :, columns] + piece if third else piece

    def wait_sent(stage, source, chunk):
        if stage == 0:
            most = circles.at[chunk, pl.ds(0, SECTORS - 1)]
        else:
            most = source.at[chunk, pl.ds(0, 15 * BLOCK)]
        pltpu.make_async_copy(most, most, sems.at[2 * stage, chunk]).wait()

    load_rows(0).wait()
    lax.fori_loop(0, SECTORS, lambda owner, _: (arrange(0, owner), 0)[1], 0)
    pl.semaphore_wait(barrier, 30)
    burst(circle_messages(0))
    keep_circle(0)
    spread_waves()
    build_matrix()
    for chunk in range(1, CHUNKS):
        load_rows(chunk).wait()
    burst(circle_messages(1))
    keep_circle(1)
    transform(0)
    burst(circle_messages(2))
    keep_circle(2)
    build_table()
    transform(1)
    burst(lat_messages(1), circle_messages(3), circle_messages(4)[:8])
    keep_block(1, 1)
    keep_circle(3)
    transform(2)
    burst(lat_messages(2), circle_messages(4)[8:] + circle_messages(5))
    keep_block(1, 2)
    keep_circle(4)
    keep_circle(5)
    transform(3)
    turn_over(0)
    burst(lat_messages(3), lon_messages(0))
    keep_block(1, 3)
    keep_block(2, 0)
    transform(4)
    transform(5)
    regroup(5)
    burst(lon_messages(5))
    keep_block(2, 5)
    turn_over(1)
    turn_over(2)
    burst(lat_messages(4), lon_messages(1) + lon_messages(2))
    keep_block(1, 4)
    keep_block(2, 1)
    keep_block(2, 2)
    sum_up(0)
    turn_late(5)
    turn_over(3)
    burst(lat_messages(5), lon_messages(3))
    keep_block(1, 5)
    keep_block(2, 3)
    sum_up(1)
    sum_up(2)
    turn_over(4)
    burst(lon_messages(4))
    keep_block(2, 4)
    sum_up(3)
    sum_up(5)
    sum_up(4)
    for chunk in range(CHUNKS):
        wait_sent(0, None, chunk)
        wait_sent(1, send_lat, chunk)
        wait_sent(2, send_lon, chunk)


def on_device(grid_values, wave_table, legendre_basis):
    any_space = pl.BlockSpec(memory_space=pl.ANY)
    vmem = pl.BlockSpec(memory_space=pltpu.VMEM)
    return pl.pallas_call(
        kernel,
        out_shape=pltpu.VMEM((2, 720, 512), jnp.float32),
        in_specs=[any_space, vmem, any_space],
        out_specs=vmem,
        scratch_shapes=[
            pltpu.VMEM((CHUNKS, 90, 16, LANES), jnp.float32),
            pltpu.VMEM((CHUNKS, SECTORS, 90, LANES), jnp.float32),
            pltpu.VMEM((CHUNKS, SECTORS, 90, LANES), jnp.float32),
            pltpu.VMEM((512, LANES), jnp.float32),
            pltpu.VMEM((ALL_ROWS, POINTS), jnp.bfloat16),
            pltpu.VMEM((ALL_ROWS, POINTS), jnp.bfloat16),
            pltpu.VMEM((POINTS, 2 * LANES), jnp.bfloat16),
            pltpu.VMEM((CHUNKS, ALL_ROWS, LANES), jnp.float32),
            pltpu.VMEM((CHUNKS, ALL_ROWS, LANES), jnp.float32),
            pltpu.VMEM((CHUNKS, ALL_ROWS, LANES), jnp.float32),
            pltpu.VMEM((CHUNKS, ALL_ROWS, LANES), jnp.float32),
            pltpu.VMEM((2, 720, 384), jnp.float32),
            pltpu.VMEM((2, THIRDS + 1, 720, 256), jnp.bfloat16),
            pltpu.VMEM((2, THIRDS + 1, 720, 256), jnp.bfloat16),
            pltpu.SemaphoreType.DMA((6, CHUNKS)),
            pltpu.SemaphoreType.DMA((3, CHUNKS)),
            pltpu.SemaphoreType.DMA((CHUNKS,)),
            pltpu.SemaphoreType.DMA,
        ],
        compiler_params=pltpu.CompilerParams(
            collective_id=0, has_side_effects=True, vmem_limit_bytes=56 * 1024 * 1024
        ),
        name="transform",
    )(jnp.swapaxes(grid_values, 0, 1), wave_table.reshape(4, LANES), jnp.swapaxes(legendre_basis, 1, 2))


def solution(mesh):
    placed = (P("lat", "lon", None), P(), P(("lat", "lon"), None, None))
    return jax.shard_map(
        on_device,
        mesh=mesh,
        in_specs=placed,
        out_specs=P(("lat", "lon"), None, None),
        check_vma=False,
    )
```

```python
import functools
import math

import jax
import jax.numpy as jnp
from jax import lax
from jax.experimental import pallas as pl
from jax.experimental.pallas import tpu as pltpu
from jax.sharding import PartitionSpec as P

CIRCLE = 1440
LANES = 128
SECTORS = 16
BANDS = 16
SECTOR_ROWS = 96
POINTS = SECTORS * SECTOR_ROWS
THIRDS = 3
HALVES = 2
CHUNKS = THIRDS * HALVES
BLOCK = 64
ALL_ROWS = 16 * BLOCK


LON_STEPS = (
    (2, 2), (2, 1), (1, 2), (2, 3), (3, 2), (1, 1), (3, 3), (1, 3), (3, 1), (2, 0), (0, 2), (1, 0), (0, 1), (3, 0), (0, 3),
)
FAR_LAT_STEPS = (
    (4, 0), (4, 1), (3, 0), (5, 1), (3, 1), (5, 0), (2, 0), (6, 1), (2, 1), (6, 0), (1, 0), (7, 1), (1, 1), (7, 0), (0, 1),
)
LAT_STEPS = (
    (1, 0), (7, 1), (2, 0), (6, 1), (3, 0), (5, 1), (4, 0), (4, 1), (7, 0), (1, 1), (6, 0), (2, 1), (5, 0), (3, 1), (0, 1),
)


def split(values):
    high = values.astype(jnp.bfloat16)
    low = (values - high.astype(jnp.float32)).astype(jnp.bfloat16)
    return high, low


def unit_circle(turns):
    half = turns * math.pi
    square = half * half
    sine = jnp.full_like(half, -1.0 / 39916800.0)
    for order in (9, 7, 5, 3, 1):
        sine = sine * square + (-1.0) ** (order // 2) / math.factorial(order)
    sine = sine * half
    cosine = jnp.full_like(half, 1.0 / 479001600.0)
    for order in (10, 8, 6, 4, 2, 0):
        cosine = cosine * square + (-1.0) ** (order // 2) / math.factorial(order)
    return 1.0 - 2.0 * sine * sine, 2.0 * sine * cosine


def fraction(product, circle):
    whole = jnp.floor(product * (1.0 / circle) + 0.5)
    return (product - whole * circle) * (1.0 / circle)


def kernel(
    grid, numbers, basis, out,
    rows_held, circles_out, circles, waves, matrix_high, matrix_low, points,
    send_lat, recv_lat, send_lon, recv_lon,
    table, table_high, table_low,
    sems, own_sems, row_sems, table_sem,
):
    lat = lax.axis_index("lat")
    lon = lax.axis_index("lon")
    northern = lat < 8
    place = jnp.where(northern, lat, 23 - lat)

    core = lax.rem(lat, 2)
    turn = 1 - 2 * core

    def lon_peer(step, way):
        x = lax.rem(lon // 4 + way * turn * step[0] + 4, 4)
        y = lax.rem(lax.rem(lon, 4) + way * turn * step[1] + 4, 4)
        return x * 4 + y

    def lat_peer(step):
        z = lax.rem(lat // 2 + turn * step[0] + 8, 8)
        return z * 2 + lax.rem(core + step[1], 2)

    def load_rows(chunk):
        half, third = divmod(chunk, THIRDS)
        first = pl.multiple_of(jnp.where(northern, 16 * third, 32 - 16 * third), 16)
        return pltpu.make_async_copy(
            grid.at[:, pl.ds(first, 16), pl.ds(half * LANES, LANES)],
            rows_held.at[chunk, pl.ds(0, 90)],
            row_sems.at[chunk],
        )

    load_rows(0).start()
    barrier = pltpu.get_barrier_semaphore()
    for lat_step, lon_step in zip(FAR_LAT_STEPS, LON_STEPS):
        pl.semaphore_signal(barrier, inc=1, device_id={"lat": lat_peer(lat_step)}, device_id_type=pl.DeviceIdType.MESH)
        pl.semaphore_signal(barrier, inc=1, device_id={"lon": lon_peer(lon_step, 1)}, device_id_type=pl.DeviceIdType.MESH)
    for chunk in range(1, CHUNKS):
        load_rows(chunk).start()
    table_copy = pltpu.make_async_copy(basis, table, table_sem)
    table_copy.start()

    def arrange(chunk, owner):
        start = jnp.where(northern, owner, 15 - owner)
        circles_out[chunk, owner] = rows_held.at[chunk].reshape(SECTOR_ROWS * 16, LANES)[pl.ds(start, 90, stride=16), :]

    def send_circle(chunk, peer):
        if chunk:
            arrange(chunk, peer)
        pltpu.make_async_remote_copy(
            src_ref=circles_out.at[chunk, peer],
            dst_ref=circles.at[chunk, lon],
            send_sem=sems.at[0, chunk],
            recv_sem=sems.at[1, chunk],
            device_id={"lon": peer},
            device_id_type=pl.DeviceIdType.MESH,
        ).start()

    def keep_circle(chunk):
        if chunk:
            arrange(chunk, lon)
        pltpu.make_async_copy(circles_out.at[chunk, lon], circles.at[chunk, lon], own_sems.at[0, chunk]).start()

    def wait_circles(chunk):
        most = circles.at[chunk, pl.ds(0, SECTORS - 1)]
        pltpu.make_async_copy(most, most, sems.at[1, chunk]).wait()
        one = circles.at[chunk, 0]
        pltpu.make_async_copy(one, one, own_sems.at[0, chunk]).wait()

    def block_copy(stage, peer, chunk):
        source, target = ((send_lat, recv_lat), (send_lon, recv_lon))[stage - 1]
        mine = (place, lon)[stage - 1]
        return (
            source.at[chunk, pl.ds(pl.multiple_of(peer * BLOCK, BLOCK), BLOCK)],
            target.at[chunk, pl.ds(pl.multiple_of(mine * BLOCK, BLOCK), BLOCK)],
        )

    def send_block(stage, peer, chunk):
        source, target = block_copy(stage, peer, chunk)
        pltpu.make_async_remote_copy(
            src_ref=source,
            dst_ref=target,
            send_sem=sems.at[2 * stage, chunk],
            recv_sem=sems.at[2 * stage + 1, chunk],
            device_id={("lat", "lon")[stage - 1]: peer},
            device_id_type=pl.DeviceIdType.MESH,
        ).start()

    def keep_block(stage, chunk):
        source, target = block_copy(stage, (lat, lon)[stage - 1], chunk)
        pltpu.make_async_copy(source, target, own_sems.at[stage, chunk]).start()

    def circle_messages(chunk):
        return [functools.partial(lambda step: send_circle(chunk, lon_peer(step, 1)), step) for step in LON_STEPS]

    def lat_messages(chunk):
        return [functools.partial(lambda step: send_block(1, lat_peer(step), chunk), step) for step in LAT_STEPS]

    def lon_messages(chunk):
        return [functools.partial(lambda step: send_block(2, lon_peer(step, -1), chunk), step) for step in LON_STEPS]

    def burst(*lists):
        order = [((place + 0.5) / len(each), index, message) for index, each in enumerate(lists) for place, message in enumerate(each)]
        for _, _, message in sorted(order, key=lambda entry: entry[:2]):
            message()

    def wait_blocks(stage, target, chunk):
        most = target.at[chunk, pl.ds(0, 15 * BLOCK)]
        pltpu.make_async_copy(most, most, sems.at[2 * stage + 1, chunk]).wait()
        one = target.at[chunk, pl.ds(0, BLOCK)]
        pltpu.make_async_copy(one, one, own_sems.at[stage, chunk]).wait()

    def spread_waves():
        for group in range(4):
            values = jnp.broadcast_to(numbers[group : group + 1, :].astype(jnp.float32), (LANES, LANES))
            waves[LANES * group : LANES * (group + 1), :] = values.T

    def build_matrix():
        lane = lax.broadcasted_iota(jnp.int32, (32, LANES), 1).astype(jnp.float32)
        factor = 1.0 / math.sqrt(CIRCLE)

        def one(block, _):
            wave = waves[pl.ds(pl.multiple_of(block * 32, 32), 32), :]
            for group in range(3):
                position = lane + float(LANES * group)
                sector = jnp.floor(position * (1.0 / 96.0) + 0.001)
                point = position - 6.0 * sector
                cosine, sine = unit_circle(fraction(wave * point, float(CIRCLE)))
                cosine, sine = cosine * factor, sine * factor
                for quarter in range(4):
                    turn = fraction(wave * float(quarter), 4.0) * 4.0
                    turn_cos = 1.0 - jnp.abs(turn)
                    turn_sin = jnp.where(turn == -2.0, 0.0, turn)
                    real = turn_cos * cosine - turn_sin * sine
                    imaginary = -turn_sin * cosine - turn_cos * sine
                    columns = pl.ds(384 * quarter + LANES * group, LANES)
                    for offset, values in ((0, real), (32, imaginary)):
                        rows = pl.ds(pl.multiple_of(block * BLOCK + offset, 32), 32)
                        matrix_high[rows, columns], matrix_low[rows, columns] = split(values)
            return 0

        lax.fori_loop(0, 16, one, 0)

    def build_table():
        table_copy.wait()
        degree = lax.broadcasted_iota(jnp.int32, (720, 256), 0).astype(jnp.float32)
        row = lax.broadcasted_iota(jnp.int32, (384, 256), 0)
        column = lax.broadcasted_iota(jnp.int32, (384, 256), 1)
        wide_column = lax.broadcasted_iota(jnp.int32, (720, 256), 1)
        first = (lat * SECTORS + lon) * 2
        for slot in range(2):
            wave = jnp.broadcast_to(waves[pl.ds(first + slot, 1), :][:, :1], (1, 256))
            sign = 1.0 - 4.0 * jnp.abs(fraction(degree + wave, 2.0))
            parts = split(table[slot])
            for kind in range(THIRDS + 1):
                if kind < THIRDS:
                    wanted = 48 * (column & 7) + (column >> 4) + 16 * kind
                    southern = (wide_column & 8) == 8
                else:
                    wanted = 48 * ((column >> 4) & 7) + (column & 15) + 16 * (THIRDS - 1)
                    southern = wide_column >= 128
                pick = jnp.where(row == wanted, 1.0, 0.0).astype(jnp.bfloat16)
                signs = jnp.where(southern, sign, 1.0)
                for part, target in zip(parts, (table_high, table_low)):
                    placed = jnp.dot(part, pick, preferred_element_type=jnp.float32)
                    target[slot, kind] = (placed * signs).astype(jnp.bfloat16)

    def transform(chunk):
        wait_circles(chunk)

        def cut(sector, _):
            values = circles[chunk, sector]
            values = jnp.concatenate([values, jnp.zeros((SECTOR_ROWS - 90, LANES), jnp.float32)], 0)
            high, low = split(values)
            rows = pl.ds(pl.multiple_of(sector * SECTOR_ROWS, SECTOR_ROWS), SECTOR_ROWS)
            points[rows, :LANES], points[rows, LANES:] = high, low
            return 0

        lax.fori_loop(0, SECTORS, cut, 0)

        def rows_of(part):
            rows = pl.ds(pl.multiple_of(part * 256, 256), 256)
            both = jnp.dot(matrix_high[rows, :], points[...], preferred_element_type=jnp.float32)
            rest = jnp.dot(matrix_low[rows, :], points[:, :LANES], preferred_element_type=jnp.float32)
            send_lat[chunk, rows, :] = both[:, :LANES] + both[:, LANES:] + rest

        if chunk:
            lax.fori_loop(0, 4, lambda part, _: (rows_of(part), 0)[1], 0)
            return
        mine = lat // 4

        def one(step, _):
            part = lax.rem(mine + turn * (1 + 2 * step - 3 * (step // 2)) + 4, 4)
            rows_of(part)
            for number in range(4):
                send_block(1, part * 4 + lax.rem(lat + number, 4), 0)
            return 0

        lax.fori_loop(0, 3, one, 0)
        rows_of(mine)
        for number in range(1, 4):
            send_block(1, mine * 4 + lax.rem(lat + number, 4), 0)
        keep_block(1, 0)

    def regroup(chunk):
        def one(owner, _):
            for slot in range(2):
                values = send_lat[chunk, pl.ds(owner * 2 + slot, 32, stride=32), :]
                send_lon[chunk, pl.ds(pl.multiple_of(owner * BLOCK + slot * 32, 32), 32), :] = values
            return 0

        lax.fori_loop(0, SECTORS, one, 0)

    def turn_late(chunk):
        wait_blocks(2, recv_lon, chunk)

        def one(owner, _):
            for slot in range(2):
                for part in range(2):
                    values = recv_lon[chunk, pl.ds(slot * 32 + owner * 2 + part, 16, stride=BLOCK), :]
                    send_lat[chunk, pl.ds(pl.multiple_of(owner * BLOCK + slot * 32 + part * 16, 16), 16), :] = values
            return 0

        lax.fori_loop(0, BANDS, one, 0)

    def turn_over(chunk):
        wait_blocks(1, recv_lat, chunk)

        def one(owner, _):
            for slot in range(2):
                for part in range(2):
                    values = recv_lat[chunk, pl.ds(part * 32 + owner * 2 + slot, 16, stride=BLOCK), :]
                    send_lon[chunk, pl.ds(pl.multiple_of(owner * BLOCK + slot * 32 + part * 16, 16), 16), :] = values
            return 0

        lax.fori_loop(0, SECTORS, one, 0)

    def sum_up(chunk):
        half, third = divmod(chunk, THIRDS)
        late = chunk == CHUNKS - 1
        if late:
            wait_blocks(1, recv_lat, chunk)
        else:
            wait_blocks(2, recv_lon, chunk)
        arrived = (recv_lat if late else recv_lon)[chunk].reshape(16, 2, 2, 16, LANES)
        for slot in range(2):
            pair = [arrived[:, slot, part].reshape(256, LANES) for part in range(2)]
            high, low = split(jnp.concatenate(pair, 1))
            kind = THIRDS if late else third
            one_high, one_low = table_high[slot, kind], table_low[slot, kind]
            sums = jnp.dot(
                jnp.concatenate([one_high, one_high, one_low], 1),
                jnp.concatenate([high, low, high], 0),
                preferred_element_type=jnp.float32,
            )
            for part in range(2):
                columns = pl.ds(part * 256 + half * LANES, LANES)
                piece = sums[:, part * LANES : (part + 1) * LANES]
                out[slot, :, columns] = out[slot, :, columns] + piece if third else piece

    def wait_sent(stage, source, chunk):
        if stage == 0:
            most = circles.at[chunk, pl.ds(0, SECTORS - 1)]
        else:
            most = source.at[chunk, pl.ds(0, 15 * BLOCK)]
        pltpu.make_async_copy(most, most, sems.at[2 * stage, chunk]).wait()

    load_rows(0).wait()
    lax.fori_loop(0, SECTORS, lambda owner, _: (arrange(0, owner), 0)[1], 0)
    pl.semaphore_wait(barrier, 30)
    burst(circle_messages(0))
    keep_circle(0)
    spread_waves()
    build_matrix()
    for chunk in range(1, CHUNKS):
        load_rows(chunk).wait()
    burst(circle_messages(1))
    keep_circle(1)
    transform(0)
    burst(circle_messages(2))
    keep_circle(2)
    build_table()
    transform(1)
    burst(lat_messages(1), circle_messages(3), circle_messages(4)[:8])
    keep_block(1, 1)
    keep_circle(3)
    transform(2)
    burst(lat_messages(2), circle_messages(4)[8:] + circle_messages(5))
    keep_block(1, 2)
    keep_circle(4)
    keep_circle(5)
    transform(3)
    turn_over(0)
    burst(lat_messages(3), lon_messages(0))
    keep_block(1, 3)
    keep_block(2, 0)
    transform(4)
    transform(5)
    regroup(5)
    burst(lon_messages(5))
    keep_block(2, 5)
    turn_over(1)
    turn_over(2)
    burst(lat_messages(4), lon_messages(1) + lon_messages(2))
    keep_block(1, 4)
    keep_block(2, 1)
    keep_block(2, 2)
    sum_up(0)
    turn_late(5)
    turn_over(3)
    burst(lat_messages(5), lon_messages(3))
    keep_block(1, 5)
    keep_block(2, 3)
    sum_up(1)
    sum_up(2)
    turn_over(4)
    burst(lon_messages(4))
    keep_block(2, 4)
    sum_up(3)
    sum_up(5)
    sum_up(4)
    for chunk in range(CHUNKS):
        wait_sent(0, None, chunk)
        wait_sent(1, send_lat, chunk)
        wait_sent(2, send_lon, chunk)


def on_device(grid_values, wave_table, legendre_basis):
    any_space = pl.BlockSpec(memory_space=pl.ANY)
    vmem = pl.BlockSpec(memory_space=pltpu.VMEM)
    return pl.pallas_call(
        kernel,
        out_shape=pltpu.VMEM((2, 720, 512), jnp.float32),
        in_specs=[any_space, vmem, any_space],
        out_specs=vmem,
        scratch_shapes=[
            pltpu.VMEM((CHUNKS, SECTOR_ROWS, 16, LANES), jnp.float32),
            pltpu.VMEM((CHUNKS, SECTORS, 90, LANES), jnp.float32),
            pltpu.VMEM((CHUNKS, SECTORS, 90, LANES), jnp.float32),
            pltpu.VMEM((520, LANES), jnp.float32),
            pltpu.VMEM((ALL_ROWS, POINTS), jnp.bfloat16),
            pltpu.VMEM((ALL_ROWS, POINTS), jnp.bfloat16),
            pltpu.VMEM((POINTS, 2 * LANES), jnp.bfloat16),
            pltpu.VMEM((CHUNKS, ALL_ROWS, LANES), jnp.float32),
            pltpu.VMEM((CHUNKS, ALL_ROWS, LANES), jnp.float32),
            pltpu.VMEM((CHUNKS, ALL_ROWS, LANES), jnp.float32),
            pltpu.VMEM((CHUNKS, ALL_ROWS, LANES), jnp.float32),
            pltpu.VMEM((2, 720, 384), jnp.float32),
            pltpu.VMEM((2, THIRDS + 1, 720, 256), jnp.bfloat16),
            pltpu.VMEM((2, THIRDS + 1, 720, 256), jnp.bfloat16),
            pltpu.SemaphoreType.DMA((6, CHUNKS)),
            pltpu.SemaphoreType.DMA((3, CHUNKS)),
            pltpu.SemaphoreType.DMA((CHUNKS,)),
            pltpu.SemaphoreType.DMA,
        ],
        compiler_params=pltpu.CompilerParams(
            collective_id=0, has_side_effects=True, vmem_limit_bytes=56 * 1024 * 1024
        ),
        name="transform",
    )(jnp.swapaxes(grid_values, 0, 1), wave_table.reshape(4, LANES), jnp.swapaxes(legendre_basis, 1, 2))


def solution(mesh):
    placed = (P("lat", "lon", None), P(), P(("lat", "lon"), None, None))
    return jax.shard_map(
        on_device,
        mesh=mesh,
        in_specs=placed,
        out_specs=P(("lat", "lon"), None, None),
        check_vma=False,
    )
```

```python
import functools
import math

import jax
import jax.numpy as jnp
from jax import lax
from jax.experimental import pallas as pl
from jax.experimental.pallas import tpu as pltpu
from jax.sharding import PartitionSpec as P

CIRCLE = 1440
LANES = 128
SECTORS = 16
BANDS = 16
SECTOR_ROWS = 96
POINTS = SECTORS * SECTOR_ROWS
THIRDS = 3
HALVES = 2
CHUNKS = THIRDS * HALVES
BLOCK = 64
ALL_ROWS = 16 * BLOCK


LON_STEPS = (
    (2, 2), (2, 1), (1, 2), (2, 3), (3, 2), (1, 1), (3, 3), (1, 3), (3, 1), (2, 0), (0, 2), (1, 0), (0, 1), (3, 0), (0, 3),
)
FAR_LAT_STEPS = (
    (4, 0), (4, 1), (3, 0), (5, 1), (3, 1), (5, 0), (2, 0), (6, 1), (2, 1), (6, 0), (1, 0), (7, 1), (1, 1), (7, 0), (0, 1),
)
LAT_STEPS = (
    (1, 0), (7, 1), (2, 0), (6, 1), (3, 0), (5, 1), (4, 0), (4, 1), (7, 0), (1, 1), (6, 0), (2, 1), (5, 0), (3, 1), (0, 1),
)


def split(values):
    high = values.astype(jnp.bfloat16)
    low = (values - high.astype(jnp.float32)).astype(jnp.bfloat16)
    return high, low


def unit_circle(turns):
    half = turns * math.pi
    square = half * half
    sine = jnp.full_like(half, -1.0 / 39916800.0)
    for order in (9, 7, 5, 3, 1):
        sine = sine * square + (-1.0) ** (order // 2) / math.factorial(order)
    sine = sine * half
    cosine = jnp.full_like(half, 1.0 / 479001600.0)
    for order in (10, 8, 6, 4, 2, 0):
        cosine = cosine * square + (-1.0) ** (order // 2) / math.factorial(order)
    return 1.0 - 2.0 * sine * sine, 2.0 * sine * cosine


def fraction(product, circle):
    whole = jnp.floor(product * (1.0 / circle) + 0.5)
    return (product - whole * circle) * (1.0 / circle)


def kernel(
    grid, numbers, basis, out,
    rows_held, circles_out, circles, waves, matrix_high, matrix_low, points,
    send_lat, recv_lat, send_lon, recv_lon,
    table, table_high, table_low,
    sems, own_sems, row_sems, table_sem,
):
    lat = lax.axis_index("lat")
    lon = lax.axis_index("lon")
    northern = lat < 8
    place = jnp.where(northern, lat, 23 - lat)

    core = lax.rem(lat, 2)
    turn = 1 - 2 * core

    def lon_peer(step, way):
        x = lax.rem(lon // 4 + way * turn * step[0] + 4, 4)
        y = lax.rem(lax.rem(lon, 4) + way * turn * step[1] + 4, 4)
        return x * 4 + y

    def lat_peer(step):
        z = lax.rem(lat // 2 + turn * step[0] + 8, 8)
        return z * 2 + lax.rem(core + step[1], 2)

    def load_rows(chunk):
        half, third = divmod(chunk, THIRDS)
        first = pl.multiple_of(jnp.where(northern, 16 * third, 32 - 16 * third), 16)
        return pltpu.make_async_copy(
            grid.at[:, pl.ds(first, 16), pl.ds(half * LANES, LANES)],
            rows_held.at[chunk, pl.ds(0, 90)],
            row_sems.at[chunk],
        )

    load_rows(0).start()
    barrier = pltpu.get_barrier_semaphore()
    for lat_step, lon_step in zip(FAR_LAT_STEPS, LON_STEPS):
        pl.semaphore_signal(barrier, inc=1, device_id={"lat": lat_peer(lat_step)}, device_id_type=pl.DeviceIdType.MESH)
        pl.semaphore_signal(barrier, inc=1, device_id={"lon": lon_peer(lon_step, 1)}, device_id_type=pl.DeviceIdType.MESH)
    for chunk in range(1, CHUNKS):
        load_rows(chunk).start()
    table_copy = pltpu.make_async_copy(basis, table, table_sem)
    table_copy.start()

    def arrange(chunk, owner):
        start = jnp.where(northern, owner, 15 - owner)
        circles_out[chunk, owner] = rows_held.at[chunk].reshape(SECTOR_ROWS * 16, LANES)[pl.ds(start, 90, stride=16), :]

    def send_circle(chunk, peer):
        if chunk:
            arrange(chunk, peer)
        pltpu.make_async_remote_copy(
            src_ref=circles_out.at[chunk, peer],
            dst_ref=circles.at[chunk, lon],
            send_sem=sems.at[0, chunk],
            recv_sem=sems.at[1, chunk],
            device_id={"lon": peer},
            device_id_type=pl.DeviceIdType.MESH,
        ).start()

    def keep_circle(chunk):
        if chunk:
            arrange(chunk, lon)
        pltpu.make_async_copy(circles_out.at[chunk, lon], circles.at[chunk, lon], own_sems.at[0, chunk]).start()

    def wait_circles(chunk):
        most = circles.at[chunk, pl.ds(0, SECTORS - 1)]
        pltpu.make_async_copy(most, most, sems.at[1, chunk]).wait()
        one = circles.at[chunk, 0]
        pltpu.make_async_copy(one, one, own_sems.at[0, chunk]).wait()

    def block_copy(stage, peer, chunk):
        source, target = ((send_lat, recv_lat), (send_lon, recv_lon))[stage - 1]
        mine = (place, lon)[stage - 1]
        return (
            source.at[chunk, pl.ds(pl.multiple_of(peer * BLOCK, BLOCK), BLOCK)],
            target.at[chunk, pl.ds(pl.multiple_of(mine * BLOCK, BLOCK), BLOCK)],
        )

    def send_block(stage, peer, chunk):
        source, target = block_copy(stage, peer, chunk)
        pltpu.make_async_remote_copy(
            src_ref=source,
            dst_ref=target,
            send_sem=sems.at[2 * stage, chunk],
            recv_sem=sems.at[2 * stage + 1, chunk],
            device_id={("lat", "lon")[stage - 1]: peer},
            device_id_type=pl.DeviceIdType.MESH,
        ).start()

    def keep_block(stage, chunk):
        source, target = block_copy(stage, (lat, lon)[stage - 1], chunk)
        pltpu.make_async_copy(source, target, own_sems.at[stage, chunk]).start()

    def circle_messages(chunk):
        return [functools.partial(lambda step: send_circle(chunk, lon_peer(step, 1)), step) for step in LON_STEPS]

    def lat_messages(chunk):
        return [functools.partial(lambda step: send_block(1, lat_peer(step), chunk), step) for step in LAT_STEPS]

    def lon_messages(chunk):
        return [functools.partial(lambda step: send_block(2, lon_peer(step, -1), chunk), step) for step in LON_STEPS]

    def burst(*lists):
        order = [((place + 0.5) / len(each), index, message) for index, each in enumerate(lists) for place, message in enumerate(each)]
        for _, _, message in sorted(order, key=lambda entry: entry[:2]):
            message()

    def wait_blocks(stage, target, chunk):
        most = target.at[chunk, pl.ds(0, 15 * BLOCK)]
        pltpu.make_async_copy(most, most, sems.at[2 * stage + 1, chunk]).wait()
        one = target.at[chunk, pl.ds(0, BLOCK)]
        pltpu.make_async_copy(one, one, own_sems.at[stage, chunk]).wait()

    def spread_waves():
        for group in range(4):
            values = jnp.broadcast_to(numbers[group : group + 1, :].astype(jnp.float32), (LANES, LANES))
            waves[LANES * group : LANES * (group + 1), :] = values.T

    def build_matrix():
        lane = lax.broadcasted_iota(jnp.int32, (32, LANES), 1).astype(jnp.float32)
        factor = 1.0 / math.sqrt(CIRCLE)

        def one(block, _):
            wave = waves[pl.ds(pl.multiple_of(block * 32, 32), 32), :]
            for group in range(3):
                position = lane + float(LANES * group)
                sector = jnp.floor(position * (1.0 / 96.0) + 0.001)
                point = position - 6.0 * sector
                cosine, sine = unit_circle(fraction(wave * point, float(CIRCLE)))
                cosine, sine = cosine * factor, sine * factor
                for quarter in range(4):
                    turn = fraction(wave * float(quarter), 4.0) * 4.0
                    turn_cos = 1.0 - jnp.abs(turn)
                    turn_sin = jnp.where(turn == -2.0, 0.0, turn)
                    real = turn_cos * cosine - turn_sin * sine
                    imaginary = -turn_sin * cosine - turn_cos * sine
                    columns = pl.ds(384 * quarter + LANES * group, LANES)
                    for offset, values in ((0, real), (32, imaginary)):
                        rows = pl.ds(pl.multiple_of(block * BLOCK + offset, 32), 32)
                        matrix_high[rows, columns], matrix_low[rows, columns] = split(values)
            return 0

        lax.fori_loop(0, 16, one, 0)

    def build_table():
        table_copy.wait()
        degree = lax.broadcasted_iota(jnp.int32, (720, 256), 0).astype(jnp.float32)
        row = lax.broadcasted_iota(jnp.int32, (384, 256), 0)
        column = lax.broadcasted_iota(jnp.int32, (384, 256), 1)
        wide_column = lax.broadcasted_iota(jnp.int32, (720, 256), 1)
        first = (lat * SECTORS + lon) * 2
        for slot in range(2):
            wave = jnp.broadcast_to(waves[pl.ds(first + slot, 1), :][:, :1], (1, 256))
            sign = 1.0 - 4.0 * jnp.abs(fraction(degree + wave, 2.0))
            parts = split(table[slot])
            for kind in range(THIRDS + 1):
                if kind < THIRDS:
                    wanted = 48 * (column & 7) + (column >> 4) + 16 * kind
                    southern = (wide_column & 8) == 8
                else:
                    wanted = 48 * ((column >> 4) & 7) + (column & 15) + 16 * (THIRDS - 1)
                    southern = wide_column >= 128
                pick = jnp.where(row == wanted, 1.0, 0.0).astype(jnp.bfloat16)
                signs = jnp.where(southern, sign, 1.0)
                for part, target in zip(parts, (table_high, table_low)):
                    placed = jnp.dot(part, pick, preferred_element_type=jnp.float32)
                    target[slot, kind] = (placed * signs).astype(jnp.bfloat16)

    def transform(chunk):
        wait_circles(chunk)

        def cut(sector, _):
            values = circles[chunk, sector]
            values = jnp.concatenate([values, jnp.zeros((SECTOR_ROWS - 90, LANES), jnp.float32)], 0)
            high, low = split(values)
            rows = pl.ds(pl.multiple_of(sector * SECTOR_ROWS, SECTOR_ROWS), SECTOR_ROWS)
            points[rows, :LANES], points[rows, LANES:] = high, low
            return 0

        lax.fori_loop(0, SECTORS, cut, 0)

        def rows_of(part):
            rows = pl.ds(pl.multiple_of(part * 256, 256), 256)
            both = jnp.dot(matrix_high[rows, :], points[...], preferred_element_type=jnp.float32)
            rest = jnp.dot(matrix_low[rows, :], points[:, :LANES], preferred_element_type=jnp.float32)
            send_lat[chunk, rows, :] = both[:, :LANES] + both[:, LANES:] + rest

        if chunk:
            lax.fori_loop(0, 4, lambda part, _: (rows_of(part), 0)[1], 0)
            return
        mine = lat // 4

        def one(step, _):
            part = lax.rem(mine + turn * (1 + 2 * step - 3 * (step // 2)) + 4, 4)
            rows_of(part)
            for number in range(4):
                send_block(1, part * 4 + lax.rem(lat + number, 4), 0)
            return 0

        lax.fori_loop(0, 3, one, 0)
        rows_of(mine)
        for number in range(1, 4):
            send_block(1, mine * 4 + lax.rem(lat + number, 4), 0)
        keep_block(1, 0)

    def regroup(chunk):
        def one(owner, _):
            for slot in range(2):
                values = send_lat[chunk, pl.ds(owner * 2 + slot, 32, stride=32), :]
                send_lon[chunk, pl.ds(pl.multiple_of(owner * BLOCK + slot * 32, 32), 32), :] = values
            return 0

        lax.fori_loop(0, SECTORS, one, 0)

    def turn_late(chunk):
        wait_blocks(2, recv_lon, chunk)

        def one(owner, _):
            for slot in range(2):
                for part in range(2):
                    values = recv_lon[chunk, pl.ds(slot * 32 + owner * 2 + part, 16, stride=BLOCK), :]
                    send_lat[chunk, pl.ds(pl.multiple_of(owner * BLOCK + slot * 32 + part * 16, 16), 16), :] = values
            return 0

        lax.fori_loop(0, BANDS, one, 0)

    def turn_over(chunk):
        wait_blocks(1, recv_lat, chunk)

        def one(owner, _):
            for slot in range(2):
                for part in range(2):
                    values = recv_lat[chunk, pl.ds(part * 32 + owner * 2 + slot, 16, stride=BLOCK), :]
                    send_lon[chunk, pl.ds(pl.multiple_of(owner * BLOCK + slot * 32 + part * 16, 16), 16), :] = values
            return 0

        lax.fori_loop(0, SECTORS, one, 0)

    def sum_up(chunk):
        half, third = divmod(chunk, THIRDS)
        late = chunk == CHUNKS - 1
        if late:
            wait_blocks(1, recv_lat, chunk)
        else:
            wait_blocks(2, recv_lon, chunk)
        arrived = (recv_lat if late else recv_lon)[chunk].reshape(16, 2, 2, 16, LANES)
        for slot in range(2):
            pair = [arrived[:, slot, part].reshape(256, LANES) for part in range(2)]
            high, low = split(jnp.concatenate(pair, 1))
            kind = THIRDS if late else third
            one_high, one_low = table_high[slot, kind], table_low[slot, kind]
            sums = jnp.dot(
                jnp.concatenate([one_high, one_high, one_low], 1),
                jnp.concatenate([high, low, high], 0),
                preferred_element_type=jnp.float32,
            )
            for part in range(2):
                columns = pl.ds(part * 256 + half * LANES, LANES)
                piece = sums[:, part * LANES : (part + 1) * LANES]
                out[slot, :, columns] = out[slot, :, columns] + piece if third else piece

    def wait_sent(stage, source, chunk):
        if stage == 0:
            most = circles.at[chunk, pl.ds(0, SECTORS - 1)]
        else:
            most = source.at[chunk, pl.ds(0, 15 * BLOCK)]
        pltpu.make_async_copy(most, most, sems.at[2 * stage, chunk]).wait()

    load_rows(0).wait()
    lax.fori_loop(0, SECTORS, lambda owner, _: (arrange(0, owner), 0)[1], 0)
    pl.semaphore_wait(barrier, 30)
    burst(circle_messages(0))
    keep_circle(0)
    spread_waves()
    build_matrix()
    for chunk in range(1, CHUNKS):
        load_rows(chunk).wait()
    burst(circle_messages(1))
    keep_circle(1)
    transform(0)
    burst(circle_messages(2))
    keep_circle(2)
    build_table()
    transform(1)
    burst(lat_messages(1), circle_messages(3))
    keep_block(1, 1)
    keep_circle(3)
    transform(2)
    burst(lat_messages(2), circle_messages(4) + circle_messages(5))
    keep_block(1, 2)
    keep_circle(4)
    keep_circle(5)
    transform(3)
    turn_over(0)
    burst(lat_messages(3), lon_messages(0))
    keep_block(1, 3)
    keep_block(2, 0)
    transform(4)
    transform(5)
    regroup(5)
    burst(lon_messages(5))
    keep_block(2, 5)
    turn_over(1)
    turn_over(2)
    burst(lat_messages(4), lon_messages(1) + lon_messages(2))
    keep_block(1, 4)
    keep_block(2, 1)
    keep_block(2, 2)
    sum_up(0)
    turn_late(5)
    turn_over(3)
    burst(lat_messages(5), lon_messages(3))
    keep_block(1, 5)
    keep_block(2, 3)
    sum_up(1)
    sum_up(2)
    turn_over(4)
    burst(lon_messages(4))
    keep_block(2, 4)
    sum_up(3)
    sum_up(5)
    for chunk in range(CHUNKS):
        wait_sent(0, None, chunk)
        wait_sent(1, send_lat, chunk)
        if chunk != 4:
            wait_sent(2, send_lon, chunk)
    sum_up(4)
    wait_sent(2, send_lon, 4)


def on_device(grid_values, wave_table, legendre_basis):
    any_space = pl.BlockSpec(memory_space=pl.ANY)
    vmem = pl.BlockSpec(memory_space=pltpu.VMEM)
    return pl.pallas_call(
        kernel,
        out_shape=pltpu.VMEM((2, 720, 512), jnp.float32),
        in_specs=[any_space, vmem, any_space],
        out_specs=vmem,
        scratch_shapes=[
            pltpu.VMEM((CHUNKS, SECTOR_ROWS, 16, LANES), jnp.float32),
            pltpu.VMEM((CHUNKS, SECTORS, 90, LANES), jnp.float32),
            pltpu.VMEM((CHUNKS, SECTORS, 90, LANES), jnp.float32),
            pltpu.VMEM((520, LANES), jnp.float32),
            pltpu.VMEM((ALL_ROWS, POINTS), jnp.bfloat16),
            pltpu.VMEM((ALL_ROWS, POINTS), jnp.bfloat16),
            pltpu.VMEM((POINTS, 2 * LANES), jnp.bfloat16),
            pltpu.VMEM((CHUNKS, ALL_ROWS, LANES), jnp.float32),
            pltpu.VMEM((CHUNKS, ALL_ROWS, LANES), jnp.float32),
            pltpu.VMEM((CHUNKS, ALL_ROWS, LANES), jnp.float32),
            pltpu.VMEM((CHUNKS, ALL_ROWS, LANES), jnp.float32),
            pltpu.VMEM((2, 720, 384), jnp.float32),
            pltpu.VMEM((2, THIRDS + 1, 720, 256), jnp.bfloat16),
            pltpu.VMEM((2, THIRDS + 1, 720, 256), jnp.bfloat16),
            pltpu.SemaphoreType.DMA((6, CHUNKS)),
            pltpu.SemaphoreType.DMA((3, CHUNKS)),
            pltpu.SemaphoreType.DMA((CHUNKS,)),
            pltpu.SemaphoreType.DMA,
        ],
        compiler_params=pltpu.CompilerParams(
            collective_id=0, has_side_effects=True, vmem_limit_bytes=56 * 1024 * 1024
        ),
        name="transform",
    )(jnp.swapaxes(grid_values, 0, 1), wave_table.reshape(4, LANES), jnp.swapaxes(legendre_basis, 1, 2))


def solution(mesh):
    placed = (P("lat", "lon", None), P(), P(("lat", "lon"), None, None))
    return jax.shard_map(
        on_device,
        mesh=mesh,
        in_specs=placed,
        out_specs=P(("lat", "lon"), None, None),
        check_vma=False,
    )
```
